512 devices in a mesh: walk: 16 (over z, core), chol: 32 (over y, x).
Axes of the slice: x: 4, y: 8, z: 8, core: 2. Of those that a mesh axis runs over, the one named last changes fastest.
Arguments:
- phi_in: float32 [768, 28672], P('walk', 'chol'), may hold values from -0.6103301 to 0.6103301
- trial: float32 [512, 56], P('chol'), may hold values from -0.176776695 to 0.176776695
- lrot: bfloat16 [28672, 2048], P('chol'), may hold values from -0.0625 to 0.0625
- fields: float32 [2, 768, 2048], P(None, 'walk', 'chol'), may hold values from -6 to 6
- src_group: int32 [768, 1], replicated, may hold values from 0 to 15; in each aligned block of 48 rows (0 to 47, 48 to 95, ...) at most 6 rows name the same one
- src_slot: int32 [768], replicated, may hold values from 0 to 47
Outputs:
- phi_out: float32 [768, 28672], P('walk', 'chol')
- fbias: float32 [768, 2048], P('walk', 'chol')
The draws below stay inside these ranges and needn't reach their ends.
Inputs may be any that keep to these rules, and one draw needn't show every extreme that they name: `src_group`: in each aligned block of 48 rows (the new walkers of one group) no group is named more than 6 times, a bound that some block reaches.
All inputs are finite; a program needn't handle non-finite values.
Results may differ from the reference program's by a relative error of at most 0.018.
Values may be sent and summed in bfloat16 or wider, within the bound.
No kernel may reach another device: no remote copies, remote signals or barrier semaphores. Data moves between devices by JAX's collectives and lax.ppermute only.
A program may use at most 64 MiB of HBM per device.

```python
import math
import jax
import jax.numpy as jnp
import numpy as np
from jax import lax

M = 512
N = 56
NCHOL = 2048
W_DEV = 48
STEPS = 2
GROUPS = 16
CAP = 6
WALKERS = 768


def common_trial(key):
    base = jax.random.normal(jax.random.fold_in(key, 11), (M, N), jnp.float32)
    return jnp.clip(base, -4.0, 4.0) / math.sqrt(M)


def draw_trial(key, part):
    return common_trial(key)


def draw_phi_in(key, part):
    trial_orbs = common_trial(key)
    walker_keys = jax.random.split(jax.random.fold_in(key, 14), WALKERS)
    orders = jax.vmap(lambda single: jax.random.permutation(single, N))(walker_keys)
    mixed = jnp.transpose(trial_orbs.T[orders], (0, 2, 1))
    gains = jax.random.uniform(jax.random.fold_in(key, 12), (WALKERS, 1, N), jnp.float32, 1.0, 2.0)
    noise = 0.02 * jnp.clip(jax.random.normal(jax.random.fold_in(key, 13), (WALKERS, M, N), jnp.float32), -4.0, 4.0)
    walkers = mixed * gains + noise
    return walkers.reshape(WALKERS, M * N)


def draw_fields(key, part):
    values = jnp.clip(3.0 * jax.random.normal(jax.random.fold_in(key, 21), (STEPS, WALKERS, NCHOL), jnp.float32), -6.0, 6.0)
    return values


def plant(array, own_key, least, high):
    shape = array.shape
    spot = [jax.random.randint(jax.random.fold_in(own_key, axis), (), 0, shape[axis]) for axis in range(len(shape))]
    array = array.at[tuple(spot)].set(least)
    longest = shape.index(max(shape))
    spot[longest] = (spot[longest] + 1) % shape[longest]
    return array.at[tuple(spot)].set(high)


def raised(entries, rng, source, target, shards_of, factor):
    def block_of(position):
        return (jnp.arange(entries.shape[position]) // (entries.shape[position] // shards_of)).reshape((-1,) + (1,) * (entries.ndim - 1 - position))

    first = jax.random.permutation(rng, shards_of)[block_of(target)]
    second = (block_of(target) + shards_of // 2) % shards_of
    return jnp.where((block_of(source) == first) | (block_of(source) == second), factor * entries, entries)


def shard_levels(stream_key, shape, pieces, low, largest):
    loudness = 1.0
    for dim, blocks in pieces:
        steps = jax.random.uniform(jax.random.fold_in(jax.random.fold_in(stream_key, 6), dim), (blocks,), jnp.float32, low / len(pieces), largest / len(pieces))
        loudness = loudness * jnp.repeat(jnp.exp(steps), shape[dim] // blocks).reshape((-1,) + (1,) * (len(shape) - 1 - dim))
    return loudness


def assign_block(key, own, number, rows, amount, top, limit, skew):
    sequence = jax.random.permutation(key, amount)
    packed, usual = portions_of(amount, rows * top, limit, skew, True), portions_of(amount, rows * top, limit, skew, False)
    places = jnp.arange(amount)

    def named(tallies, turn):
        used = int((tallies > 0).sum())
        fixed = max(1, used // 4)
        passed = fixed + (places - fixed + turn * (used - fixed)) % max(1, amount - fixed)
        return jnp.zeros((amount,), jnp.int32).at[sequence[jnp.where(places < fixed, places, passed)]].set(jnp.asarray(tallies, jnp.int32))

    tallies = jnp.where(number % 4 == 0, named(packed, number // 4), named(usual, number - number // 4 - 1))
    mixed = jax.random.permutation(jax.random.fold_in(own, 3), amount)
    donor, sink = mixed[0:amount // 2 * 2:2], mixed[1:amount // 2 * 2:2]
    room = jnp.minimum(tallies[donor] - 1, limit - tallies[sink]) // 2
    room = jnp.where((donor == sequence[0]) | (sink == sequence[0]) | (tallies[sink] == 0), 0, jnp.maximum(room, 0))
    passed = jax.random.randint(jax.random.fold_in(own, 4), (amount // 2,), 0, 1 << 20) % (room + 1)
    tallies = tallies.at[donor].add(-passed).at[sink].add(passed)
    items = jnp.searchsorted(jnp.cumsum(tallies), jnp.arange(rows * top), side="right").astype(jnp.int32)
    listing = items.reshape(top, rows).T
    listing = listing[jax.random.permutation(jax.random.fold_in(own, 1), rows)]
    turn = jax.random.randint(jax.random.fold_in(own, 2), (rows, 1), 0, top)
    return jnp.take_along_axis(listing, (jnp.arange(top)[None, :] + turn) % top, axis=1)


def portions_of(count, total, limit, lean, full):
    portions = [(1 << 20) // math.isqrt(rank ** lean) + 1 for rank in range(1, count + 1)]
    largest = limit if full else min(limit, max(-(-total // count), total * portions[0] // sum(portions)))
    least = 1 if total - largest >= count - 1 else 0
    holding, rest = [largest] + [least] * (count - 1), total - largest - least * (count - 1)
    while rest > 0:
        candidates = [i for i in range(1, count) if holding[i] < largest] or [i for i in range(1, count) if holding[i] < limit]
        pool, budget = sum([portions[i] for i in candidates]), rest
        for i in candidates:
            addition = min(limit - holding[i], max(1, budget * portions[i] // pool), rest)
            holding[i] = holding[i] + addition
            rest = rest - addition
    return np.array(holding)


def heavy_noise(rng, extent, width, reach, cuts, heavy, held_as=jnp.bfloat16):
    array = width * jax.random.normal(rng, extent, jnp.float32)
    if cuts:
        array = array * shard_levels(rng, extent, cuts, -0.22, 0.18)
    return jnp.clip(raised(array, jax.random.fold_in(rng, 3), *heavy), -reach, reach).astype(held_as)


def setup_inputs(seed: int = 0) -> dict:
    seeds = jax.random.split(jax.random.key(seed), 7)
    phi_in = draw_phi_in(jax.random.fold_in(seeds[6], 71), 0)
    trial = draw_trial(jax.random.fold_in(seeds[6], 71), 0)
    lrot = heavy_noise(seeds[2], (M * N, NCHOL), (M * N) ** -0.5, 0.0625, ((0, 32),), (0, 1, 32, 2.75))
    fields = draw_fields(jax.random.fold_in(seeds[6], 71), 0)
    src_group_keys = jax.random.split(jax.random.fold_in(seeds[4], 1), WALKERS // W_DEV)
    src_group_turns = jax.random.permutation(jax.random.fold_in(seeds[4], 3), WALKERS // W_DEV)
    src_group = jax.vmap(lambda own, number: assign_block(jax.random.fold_in(seeds[4], 2), own, number, W_DEV, GROUPS, 1, CAP, 2))(src_group_keys, src_group_turns).reshape((WALKERS, 1))
    src_slot = plant(jax.random.randint(seeds[5], (WALKERS,), 0, W_DEV), jax.random.fold_in(seeds[5], 1), 0, W_DEV - 1).astype(jnp.int32)
    return dict(phi_in=phi_in, trial=trial, lrot=lrot, fields=fields, src_group=src_group, src_slot=src_slot)


def invert_correlation(correlation):
    gram_matrix = jnp.einsum('wki,wkj->wij', correlation, correlation, precision=lax.Precision.HIGHEST)
    factor = jnp.linalg.cholesky(gram_matrix)

    def solve_one(lower, matrix):
        return jax.scipy.linalg.cho_solve((lower, True), matrix.T)
    return jax.vmap(solve_one)(factor, correlation)

def reference(phi_in, trial, lrot, fields, src_group, src_slot):
    source = (src_group[:, 0] * W_DEV + src_slot).astype(jnp.int32)
    walkers = phi_in[source].reshape(WALKERS, M, N)
    capped = jnp.zeros((WALKERS, NCHOL), jnp.float32)
    for step_index in range(STEPS):
        correlation = jnp.einsum('ai,waj->wij', trial, walkers, precision=lax.Precision.HIGHEST)
        inverse = invert_correlation(correlation)
        theta_half = jnp.einsum('wak,wkj->waj', walkers, inverse, precision=lax.Precision.HIGHEST)
        theta_half = theta_half.astype(jnp.bfloat16).reshape(WALKERS, M * N)
        force_sum = jnp.dot(theta_half.astype(jnp.float32), lrot.astype(jnp.float32), preferred_element_type=jnp.float32)
        capped = jnp.clip(20.0 * force_sum, -1.0, 1.0)
        drive_field = (fields[step_index] - capped).astype(jnp.bfloat16)
        push_term = jnp.dot(drive_field.astype(jnp.float32), lrot.T.astype(jnp.float32), preferred_element_type=jnp.float32).reshape(WALKERS, M, N)
        walkers = walkers + 0.03 * jnp.einsum('wai,wij->waj', push_term, correlation, precision=lax.Precision.HIGHEST)
    return (walkers.reshape(WALKERS, M * N), capped)
```

```python
import jax
import jax.numpy as jnp
from jax import lax
from jax.experimental import pallas as pl
from jax.experimental.pallas import tpu as pltpu
from jax.sharding import PartitionSpec as P

F32 = jnp.float32
BF16 = jnp.bfloat16
LANES = 128
HALF = 64
ELECS = 56
ORBS = 16
TILES = 7
DEVS = 32
WALKERS = 48
OWNERS = 24
CAP = 6
CHOLS = 2048
TAU = 0.03
EXACT = lax.Precision.HIGHEST


def vmem(count=1):
    return [pl.BlockSpec(memory_space=pltpu.VMEM)] * count


def smem():
    return [pl.BlockSpec(memory_space=pltpu.SMEM)]


def lane_ids(rows):
    return lax.broadcasted_iota(jnp.int32, (rows, LANES), 1)


def turn(block, shift):
    shift = shift % LANES
    return pltpu.roll(block, shift, 1) if shift else block


def exact_dot(left, right, left_dim, right_dim):
    return lax.dot_general(
        left, right, (((left_dim,), (right_dim,)), ((), ())),
        precision=EXACT, preferred_element_type=F32,
    )


def take_orbital(tiles, orbital, dest, lanes):
    tile, offset = divmod(orbital * ELECS, LANES)
    shift = dest - offset
    low = turn(tiles[tile], shift)
    if offset + ELECS <= LANES:
        return low
    return jnp.where(lanes >= dest + LANES - offset, turn(tiles[tile + 1], shift), low)


def pack_pair(first, second, lanes):
    blocks = []
    for orbital in range(ORBS):
        left = take_orbital(first, orbital, 0, lanes)
        right = take_orbital(second, orbital, HALF, lanes)
        block = jnp.where(lanes < HALF, left, right)
        blocks.append(jnp.where((lanes & (HALF - 1)) < ELECS, block, 0.0))
    return blocks


def unpack_tile(blocks, tile, half, lanes):
    start = tile * LANES
    result = None
    for orbital in range(start // ELECS, (start + LANES - 1) // ELECS + 1):
        moved = turn(blocks[orbital], orbital * ELECS - start - half * HALF)
        if result is None:
            result = moved
        else:
            result = jnp.where(lanes >= orbital * ELECS - start, moved, result)
    return result


def block_diagonal(pair, lanes):
    return jnp.concatenate(
        [jnp.where(lanes < HALF, pair, 0.0), jnp.where(lanes >= HALF, pair, 0.0)], axis=0
    )


def invert_pair(gram):
    lanes = lane_ids(ELECS)
    row_ids = lax.broadcasted_iota(jnp.int32, (ELECS, LANES), 0)
    within = lanes & (HALF - 1)
    for k in range(ELECS):
        column = jnp.where(
            lanes < HALF,
            jnp.broadcast_to(gram[:, k:k + 1], (ELECS, LANES)),
            jnp.broadcast_to(gram[:, HALF + k:HALF + k + 1], (ELECS, LANES)),
        )
        pivot = column[k:k + 1, :]
        row = jnp.where(within[k:k + 1, :] == k, 1.0, gram[k:k + 1, :]) / pivot
        gram = jnp.where(within == k, 0.0, gram) - column * row
        gram = jnp.where(row_ids == k, jnp.broadcast_to(row, (ELECS, LANES)), gram)
    return gram


def correlate(trial, walkers):
    rows = DEVS * ORBS // 2
    low = exact_dot(trial, walkers[:rows], 0, 0)
    high = exact_dot(trial, walkers[rows:], 0, 0)
    return low[:HALF] + high[HALF:]


def theta_blocks(walkers, correlation):
    lanes = lane_ids(HALF)
    gram = exact_dot(correlation, correlation, 0, 0)
    packed = jnp.where(lanes[:ELECS] < HALF, gram[:ELECS], gram[HALF:HALF + ELECS])
    inverse_gram = invert_pair(packed)
    inverse_gram = jnp.concatenate([inverse_gram, jnp.zeros((HALF - ELECS, LANES), F32)], axis=0)
    inverse = exact_dot(block_diagonal(inverse_gram, lanes), block_diagonal(correlation, lanes), 1, 1)
    theta = exact_dot(walkers, inverse, 1, 0)
    return [theta[DEVS * a:DEVS * (a + 1)] for a in range(ORBS)]


def migrate_pack(table_ref, phi_ref, out_ref, rows_ref):
    for tile in range(TILES):
        rows_ref[:, tile, :] = phi_ref[:, tile * LANES:(tile + 1) * LANES]
    rows_ref[:, TILES, :] = jnp.zeros((WALKERS, LANES), F32)
    for j in range(out_ref.shape[0]):
        out_ref[j] = rows_ref[table_ref[j]]


def owner_pack(place_ref, rows_ref, trial_ref, out_ref, pad_ref):
    pad_ref[...] = jnp.zeros_like(pad_ref)
    pad_ref[:, :ELECS] = trial_ref[...]
    trial = pad_ref[0:8, :] + turn(pad_ref[8:16, :], HALF)
    for d in range(DEVS):
        if d < OWNERS:
            out_ref[d, 0:8, :] = rows_ref[place_ref[d]]
            out_ref[d, 8:16, :] = rows_ref[place_ref[d + OWNERS]]
        else:
            out_ref[d, 0:16, :] = jnp.zeros((16, LANES), F32)
        out_ref[d, 16:24, :] = trial


def store_theta(theta, wide_ref, out_ref):
    lanes = lane_ids(DEVS)
    for half in range(2):
        for tile in range(TILES):
            wide_ref[:, 8 * half + tile, :] = unpack_tile(theta, tile, half, lanes)
        wide_ref[:, 8 * half + TILES, :] = jnp.zeros((DEVS, LANES), F32)
    out_ref[:, 0:16, :] = wide_ref[...].astype(BF16)


def owner_first(in_ref, theta_ref, phi_ref, corr_ref, trial_ref, wide_ref):
    lanes = lane_ids(DEVS)
    tiles = [[in_ref[:, 8 * h + k, :] for k in range(TILES)] for h in range(2)]
    walkers = jnp.concatenate(pack_pair(tiles[0], tiles[1], lanes), axis=0)
    trial = jnp.concatenate([in_ref[:, 16 + k, :] for k in range(8)], axis=0)
    correlation = correlate(trial, walkers)
    phi_ref[...] = walkers
    corr_ref[...] = correlation
    trial_ref[...] = trial
    store_theta(theta_blocks(walkers, correlation), wide_ref, theta_ref)


def owner_next(push_ref, phi_ref, corr_ref, trial_ref, out_ref, wide_ref):
    lanes = lane_ids(DEVS)
    tiles = [[push_ref[:, 8 * h + k, :] for k in range(TILES)] for h in range(2)]
    push = jnp.concatenate(pack_pair(tiles[0], tiles[1], lanes), axis=0)
    old = block_diagonal(corr_ref[...], lane_ids(HALF))
    walkers = phi_ref[...] + TAU * exact_dot(push, old, 1, 0)
    correlation = correlate(trial_ref[...], walkers)
    theta = theta_blocks(walkers, correlation)
    store_theta(theta, wide_ref, out_ref)
    blocks = [walkers[DEVS * a:DEVS * (a + 1)] for a in range(ORBS)]
    for half in range(2):
        for tile in range(TILES):
            wide_ref[:, 8 * half + tile, :] = unpack_tile(blocks, tile, half, lanes)
    high = wide_ref[...].astype(BF16)
    out_ref[:, 16:32, :] = high
    out_ref[:, 32:48, :] = (wide_ref[...] - high.astype(F32)).astype(BF16)
    sent = correlation.astype(BF16)
    for d in range(DEVS):
        out_ref[d, 48:112, :] = sent


def force_kernel(theta_ref, lrot_ref, out_ref, wide_ref):
    wide_ref[...] = theta_ref[0:OWNERS, 0:16, :].astype(F32)
    theta = jnp.concatenate(
        [
            jnp.concatenate([wide_ref[:, 8 * h + k, :] for k in range(TILES)], axis=1)
            for h in range(2)
        ],
        axis=0,
    ).astype(BF16)
    force = jnp.dot(theta, lrot_ref[...], preferred_element_type=F32)
    force = jnp.concatenate([force, jnp.zeros((16, CHOLS), F32)], axis=0)
    lanes = lane_ids(32)
    for pair in range(DEVS // 2):
        block = force[:, pair * LANES:(pair + 1) * LANES]
        top, low = block[:32], block[32:]
        out_ref[2 * pair] = jnp.where(lanes < HALF, top, turn(low, HALF)).astype(BF16)
        out_ref[2 * pair + 1] = jnp.where(lanes < HALF, turn(top, HALF), low).astype(BF16)


def drive_kernel(step, force_ref, fields_ref, out_ref, capped_ref, pad_ref):
    total = force_ref[0].astype(F32)
    for c in range(1, DEVS):
        total = total + force_ref[c].astype(F32)
    capped = jnp.clip(20.0 * total, -1.0, 1.0)
    pad_ref[...] = jnp.zeros_like(pad_ref)
    pad_ref[0:WALKERS, 0:HALF] = fields_ref[step]
    lanes = lane_ids(32)
    fields = jnp.where(lanes < HALF, pad_ref[0:32, :], turn(pad_ref[32:64, :], HALF))
    drive = (fields - capped).astype(BF16)
    for d in range(DEVS):
        out_ref[d] = drive
    capped_ref[0:32, :] = capped[:, 0:HALF]
    capped_ref[32:WALKERS, :] = turn(capped, HALF)[0:WALKERS - 32, 0:HALF]


def gather_push(drive_ref, lrot_ref):
    lanes = lane_ids(32)
    tops, lows = [], []
    for pair in range(DEVS // 2):
        left = drive_ref[2 * pair].astype(F32)
        right = drive_ref[2 * pair + 1].astype(F32)
        tops.append(jnp.where(lanes < HALF, left, turn(right, HALF)))
        lows.append(jnp.where(lanes < HALF, turn(left, HALF), right)[0:16])
    drive = jnp.concatenate(
        [jnp.concatenate(tops, axis=1), jnp.concatenate(lows, axis=1)], axis=0
    ).astype(BF16)
    return lax.dot_general(
        drive, lrot_ref[...], (((1,), (1,)), ((), ())), preferred_element_type=F32
    )


def push_kernel(drive_ref, lrot_ref, out_ref):
    push = gather_push(drive_ref, lrot_ref)
    for half in range(2):
        rows = push[OWNERS * half:OWNERS * (half + 1)]
        for tile in range(TILES):
            out_ref[0:OWNERS, 8 * half + tile, :] = rows[:, tile * LANES:(tile + 1) * LANES]
        out_ref[0:OWNERS, 8 * half + TILES, :] = jnp.zeros((OWNERS, LANES), F32)
    out_ref[OWNERS:, :, :] = jnp.zeros((DEVS - OWNERS, 16, LANES), F32)


def last_kernel(drive_ref, lrot_ref, bundle_ref, out_ref, push_ref, wide_ref):
    push = gather_push(drive_ref, lrot_ref)
    lanes = lane_ids(OWNERS)
    tiles = [
        [
            push[OWNERS * h:OWNERS * (h + 1), k * LANES:(k + 1) * LANES]
            for k in range(TILES)
        ]
        for h in range(2)
    ]
    blocks = pack_pair(tiles[0], tiles[1], lanes)
    for orbital in range(ORBS):
        push_ref[:, orbital, :] = blocks[orbital]
    square = lane_ids(HALF)
    for d in range(OWNERS):
        pair = block_diagonal(bundle_ref[d, 48:112, :].astype(F32), square).astype(BF16)
        rows = push_ref[d]
        high = rows.astype(BF16)
        low = (rows - high.astype(F32)).astype(BF16)
        push_ref[d] = TAU * (
            jnp.dot(high, pair, preferred_element_type=F32)
            + jnp.dot(low, pair, preferred_element_type=F32)
        )
    moved = [push_ref[:, orbital, :] for orbital in range(ORBS)]
    wide_ref[...] = bundle_ref[0:OWNERS, 16:32, :].astype(F32) + bundle_ref[0:OWNERS, 32:48, :].astype(F32)
    for half in range(2):
        for tile in range(TILES):
            out_ref[OWNERS * half:OWNERS * (half + 1), tile * LANES:(tile + 1) * LANES] = (
                wide_ref[:, 8 * half + tile, :] + unpack_tile(moved, tile, half, lanes)
            )


def call(kernel, name, shapes, operands, in_specs, scratch=(), limit=48):
    single = not isinstance(shapes, (list, tuple))
    listed = [shapes] if single else list(shapes)
    result = pl.pallas_call(
        kernel,
        out_shape=listed,
        in_specs=in_specs,
        out_specs=vmem(len(listed)),
        scratch_shapes=list(scratch),
        compiler_params=pltpu.CompilerParams(vmem_limit_bytes=limit * 1024 * 1024),
        name=name,
    )(*operands)
    return result[0] if single else result


def shape(dims, dtype=F32):
    return jax.ShapeDtypeStruct(dims, dtype)


def exchange(array, axis):
    flat = array.reshape(-1, LANES)
    return lax.all_to_all(flat, axis, 0, 0, tiled=True).reshape(array.shape)


def tables(src_group, src_slot, groups, own_group, cap):
    source = src_group.reshape(groups, WALKERS)
    slots = src_slot.reshape(groups, WALKERS)
    order = jnp.arange(WALKERS, dtype=jnp.int32)
    earlier = (source[:, None, :] == source[:, :, None]) & (order[None, None, :] < order[None, :, None])
    rank = jnp.sum(earlier.astype(jnp.int32), axis=2)
    picked = (source == own_group)[:, None, :] & (
        rank[:, None, :] == jnp.arange(cap, dtype=jnp.int32)[None, :, None]
    )
    send = jnp.sum(jnp.where(picked, slots[:, None, :], 0), axis=2).reshape(groups * cap)
    own_source = lax.dynamic_index_in_dim(source, own_group, 0, keepdims=False)
    own_rank = lax.dynamic_index_in_dim(rank, own_group, 0, keepdims=False)
    return send.astype(jnp.int32), (own_source * cap + own_rank).astype(jnp.int32)


def body(phi_in, trial, lrot, fields, src_group, src_slot, cap=CAP):
    groups = lax.axis_size("walk")
    send, place = tables(src_group, src_slot, groups, lax.axis_index("walk"), cap)
    rows = call(
        migrate_pack, "migrate_pack", shape((groups * cap, 8, LANES)), (send, phi_in),
        smem() + vmem(), [pltpu.VMEM((WALKERS, 8, LANES), F32)],
    )
    rows = exchange(rows, "walk")
    owned = call(
        owner_pack, "owner_pack", shape((DEVS, 24, LANES)), (place, rows, trial),
        smem() + vmem(2), [pltpu.VMEM((ORBS, LANES), F32)],
    )
    owned = exchange(owned, "chol")
    wide = pltpu.VMEM((DEVS, 16, LANES), F32)
    few = pltpu.VMEM((OWNERS, 16, LANES), F32)
    theta, phi, corr, trial_all = call(
        owner_first, "owner_first",
        [
            shape((DEVS, 16, LANES), BF16), shape((DEVS * ORBS, LANES)),
            shape((HALF, LANES)), shape((DEVS * ORBS // 2, LANES)),
        ],
        (owned,), vmem(), [wide],
    )
    theta = exchange(theta, "chol")

    def forces(theta, step):
        force = call(
            force_kernel, "force", shape((DEVS, 32, LANES), BF16), (theta, lrot), vmem(2), [few]
        )
        force = exchange(force, "chol")
        drive, capped = call(
            lambda *refs: drive_kernel(step, *refs), "drive",
            [shape((DEVS, 32, LANES), BF16), shape((WALKERS, HALF))],
            (force, fields), vmem(2), [pltpu.VMEM((64, LANES), F32)],
        )
        return exchange(drive, "chol"), capped

    drive, _ = forces(theta, 0)
    push = call(push_kernel, "push", shape((DEVS, 16, LANES)), (drive, lrot), vmem(2))
    push = exchange(push, "chol")
    bundle = call(
        owner_next, "owner_next", shape((DEVS, 112, LANES), BF16),
        (push, phi, corr, trial_all), vmem(4), [wide],
    )
    bundle = exchange(bundle, "chol")
    drive, capped = forces(bundle, 1)
    phi_out = call(
        last_kernel, "last", shape((WALKERS, ORBS * ELECS)), (drive, lrot, bundle), vmem(3),
        [few, few],
    )
    return phi_out, capped


def solution(mesh):
    return jax.shard_map(
        body,
        mesh=mesh,
        in_specs=(
            P("walk", "chol"),
            P("chol", None),
            P("chol", None),
            P(None, "walk", "chol"),
            P(),
            P(),
        ),
        out_specs=(P("walk", "chol"), P("walk", "chol")),
        check_vma=False,
    )
```

```python
import jax
import jax.numpy as jnp
from jax import lax
from jax.experimental import pallas as pl
from jax.experimental.pallas import tpu as pltpu
from jax.sharding import PartitionSpec as P

F32 = jnp.float32
BF16 = jnp.bfloat16
LANES = 128
HALF = 64
ELECS = 56
ORBS = 16
TILES = 7
DEVS = 32
WALKERS = 48
OWNERS = 24
CAP = 6
PANEL = 8
CHOLS = 2048
TAU = 0.03
EXACT = lax.Precision.HIGHEST


def vmem(count=1):
    return [pl.BlockSpec(memory_space=pltpu.VMEM)] * count


def smem():
    return [pl.BlockSpec(memory_space=pltpu.SMEM)]


def lane_ids(rows):
    return lax.broadcasted_iota(jnp.int32, (rows, LANES), 1)


def turn(block, shift):
    shift = shift % LANES
    return pltpu.roll(block, shift, 1) if shift else block


def exact_dot(left, right, left_dim, right_dim):
    return lax.dot_general(
        left, right, (((left_dim,), (right_dim,)), ((), ())),
        precision=EXACT, preferred_element_type=F32,
    )


def take_orbital(tiles, orbital, dest, lanes):
    tile, offset = divmod(orbital * ELECS, LANES)
    shift = dest - offset
    low = turn(tiles[tile], shift)
    if offset + ELECS <= LANES:
        return low
    return jnp.where(lanes >= dest + LANES - offset, turn(tiles[tile + 1], shift), low)


def pack_pair(first, second, lanes):
    blocks = []
    for orbital in range(ORBS):
        left = take_orbital(first, orbital, 0, lanes)
        right = take_orbital(second, orbital, HALF, lanes)
        block = jnp.where(lanes < HALF, left, right)
        blocks.append(jnp.where((lanes & (HALF - 1)) < ELECS, block, 0.0))
    return blocks


def unpack_tile(blocks, tile, half, lanes):
    start = tile * LANES
    result = None
    for orbital in range(start // ELECS, (start + LANES - 1) // ELECS + 1):
        moved = turn(blocks[orbital], orbital * ELECS - start - half * HALF)
        if result is None:
            result = moved
        else:
            result = jnp.where(lanes >= orbital * ELECS - start, moved, result)
    return result


def block_diagonal(pair, lanes):
    return jnp.concatenate(
        [jnp.where(lanes < HALF, pair, 0.0), jnp.where(lanes >= HALF, pair, 0.0)], axis=0
    )


def invert_pair(gram):
    lanes = lane_ids(ELECS)
    row_ids = lax.broadcasted_iota(jnp.int32, (ELECS, LANES), 0)
    within = lanes & (HALF - 1)
    base = lanes & HALF
    for start in range(0, ELECS, PANEL):
        columns = {
            m: jnp.take_along_axis(gram, base + m, axis=1) for m in range(start, start + PANEL)
        }
        for k in range(start, start + PANEL):
            column = columns.pop(k)
            scale = 1.0 / column[k:k + 1, :]
            row = jnp.where(within[0:1] == k, 1.0, gram[k:k + 1, :]) * scale
            for m in columns:
                entry = columns[m][k:k + 1, :] * scale
                columns[m] = jnp.where(row_ids == k, entry, columns[m] - column * entry)
            gram = jnp.where(row_ids == k, row, jnp.where(within == k, 0.0, gram) - column * row)
    return gram


def correlate(trial, walkers):
    rows = DEVS * ORBS // 2
    low = exact_dot(trial, walkers[:rows], 0, 0)
    high = exact_dot(trial, walkers[rows:], 0, 0)
    return low[:HALF] + high[HALF:]


def theta_blocks(walkers, correlation):
    lanes = lane_ids(HALF)
    gram = exact_dot(correlation, correlation, 0, 0)
    packed = jnp.where(lanes[:ELECS] < HALF, gram[:ELECS], gram[HALF:HALF + ELECS])
    inverse_gram = invert_pair(packed)
    inverse_gram = jnp.concatenate([inverse_gram, jnp.zeros((HALF - ELECS, LANES), F32)], axis=0)
    inverse = exact_dot(block_diagonal(inverse_gram, lanes), block_diagonal(correlation, lanes), 1, 1)
    theta = exact_dot(walkers, inverse, 1, 0)
    return [theta[DEVS * a:DEVS * (a + 1)] for a in range(ORBS)]


def migrate_pack(group_ref, source_ref, slot_ref, phi_ref, out_ref):
    count = source_ref.shape[1]
    groups = count // WALKERS
    cap = out_ref.shape[0] // groups
    walker = lax.broadcasted_iota(jnp.int32, (8, count), 1)
    block = lax.div(walker, WALKERS)
    place = walker - block * WALKERS
    mine = jnp.broadcast_to((source_ref[...] == group_ref[0]).astype(jnp.int32), (8, count))
    order = mine
    step = 1
    while step < WALKERS:
        order = order + jnp.where(place >= step, pltpu.roll(order, step, 1), 0)
        step *= 2
    target = jnp.where(mine == 1, block * cap + order - 1, -1)[0:1]
    row_ids = lax.broadcasted_iota(jnp.int32, (groups * cap, count), 0)
    slot_ids = lax.broadcasted_iota(jnp.int32, (WALKERS, count), 0)
    taken = jnp.where(row_ids == target, 1.0, 0.0).astype(BF16)
    held = jnp.where(slot_ids == slot_ref[...], 1.0, 0.0).astype(BF16)
    choice = lax.dot_general(taken, held, (((1,), (1,)), ((), ())), preferred_element_type=F32)
    rows = exact_dot(choice, phi_ref[...], 1, 0)
    for tile in range(TILES):
        out_ref[:, tile, :] = rows[:, tile * LANES:(tile + 1) * LANES]
    out_ref[:, TILES, :] = jnp.zeros((groups * cap, LANES), F32)


def owner_pack(place_ref, rows_ref, trial_ref, out_ref, pad_ref):
    pad_ref[...] = jnp.zeros_like(pad_ref)
    pad_ref[:, :ELECS] = trial_ref[...]
    trial = pad_ref[0:8, :] + turn(pad_ref[8:16, :], HALF)
    for d in range(DEVS):
        if d < OWNERS:
            out_ref[d, 0:8, :] = rows_ref[place_ref[d]]
            out_ref[d, 8:16, :] = rows_ref[place_ref[d + OWNERS]]
        else:
            out_ref[d, 0:16, :] = jnp.zeros((16, LANES), F32)
        out_ref[d, 16:24, :] = trial


def store_walkers(blocks, first, wide_ref, out_ref):
    lanes = lane_ids(DEVS)
    for half in range(2):
        for tile in range(TILES):
            wide_ref[:, 8 * half + tile, :] = unpack_tile(blocks, tile, half, lanes)
        wide_ref[:, 8 * half + TILES, :] = jnp.zeros((DEVS, LANES), F32)
    out_ref[:, first:first + 16, :] = wide_ref[...].astype(BF16)


def owner_first(in_ref, theta_ref, phi_ref, corr_ref, trial_ref, wide_ref):
    lanes = lane_ids(DEVS)
    tiles = [[in_ref[:, 8 * h + k, :] for k in range(TILES)] for h in range(2)]
    walkers = jnp.concatenate(pack_pair(tiles[0], tiles[1], lanes), axis=0)
    trial = jnp.concatenate([in_ref[:, 16 + k, :] for k in range(8)], axis=0)
    correlation = correlate(trial, walkers)
    phi_ref[...] = walkers
    corr_ref[...] = correlation
    trial_ref[...] = trial
    store_walkers(theta_blocks(walkers, correlation), 0, wide_ref, theta_ref)


def owner_next(push_ref, phi_ref, corr_ref, trial_ref, out_ref, wide_ref):
    lanes = lane_ids(DEVS)
    wide_ref[...] = push_ref[...].astype(F32)
    tiles = [[wide_ref[:, 8 * h + k, :] for k in range(TILES)] for h in range(2)]
    push = jnp.concatenate(pack_pair(tiles[0], tiles[1], lanes), axis=0)
    old = block_diagonal(corr_ref[...], lane_ids(HALF))
    walkers = phi_ref[...] + TAU * exact_dot(push, old, 1, 0)
    correlation = correlate(trial_ref[...], walkers)
    store_walkers(theta_blocks(walkers, correlation), 0, wide_ref, out_ref)
    blocks = [walkers[DEVS * a:DEVS * (a + 1)] for a in range(ORBS)]
    store_walkers(blocks, 16, wide_ref, out_ref)
    sent = correlation.astype(BF16)
    for d in range(DEVS):
        out_ref[d, 32:96, :] = sent


def force_kernel(theta_ref, lrot_ref, out_ref, wide_ref):
    wide_ref[...] = theta_ref[0:OWNERS, 0:16, :].astype(F32)
    theta = jnp.concatenate(
        [
            jnp.concatenate([wide_ref[:, 8 * h + k, :] for k in range(TILES)], axis=1)
            for h in range(2)
        ],
        axis=0,
    ).astype(BF16)
    force = jnp.dot(theta, lrot_ref[...], preferred_element_type=F32)
    lanes = lane_ids(OWNERS)
    for pair in range(DEVS // 2):
        block = force[:, pair * LANES:(pair + 1) * LANES]
        top, low = block[:OWNERS], block[OWNERS:]
        out_ref[2 * pair] = jnp.where(lanes < HALF, top, turn(low, HALF)).astype(BF16)
        out_ref[2 * pair + 1] = jnp.where(lanes < HALF, turn(top, HALF), low).astype(BF16)


def drive_kernel(step, force_ref, fields_ref, out_ref, capped_ref, pad_ref):
    total = force_ref[0].astype(F32)
    for c in range(1, DEVS):
        total = total + force_ref[c].astype(F32)
    capped = jnp.clip(20.0 * total, -1.0, 1.0)
    pad_ref[...] = jnp.zeros_like(pad_ref)
    pad_ref[:, 0:HALF] = fields_ref[step]
    lanes = lane_ids(OWNERS)
    fields = jnp.where(lanes < HALF, pad_ref[0:OWNERS, :], turn(pad_ref[OWNERS:, :], HALF))
    drive = (fields - capped).astype(BF16)
    for d in range(DEVS):
        out_ref[d] = drive
    capped_ref[0:OWNERS, :] = capped[:, 0:HALF]
    capped_ref[OWNERS:, :] = turn(capped, HALF)[:, 0:HALF]


def gather_push(drive_ref, lrot_ref):
    lanes = lane_ids(OWNERS)
    tops, lows = [], []
    for pair in range(DEVS // 2):
        left = drive_ref[2 * pair].astype(F32)
        right = drive_ref[2 * pair + 1].astype(F32)
        tops.append(jnp.where(lanes < HALF, left, turn(right, HALF)))
        lows.append(jnp.where(lanes < HALF, turn(left, HALF), right))
    drive = jnp.concatenate(
        [jnp.concatenate(tops, axis=1), jnp.concatenate(lows, axis=1)], axis=0
    ).astype(BF16)
    return lax.dot_general(
        drive, lrot_ref[...], (((1,), (1,)), ((), ())), preferred_element_type=F32
    )


def push_kernel(drive_ref, lrot_ref, out_ref, wide_ref):
    push = gather_push(drive_ref, lrot_ref)
    for half in range(2):
        rows = push[OWNERS * half:OWNERS * (half + 1)]
        for tile in range(TILES):
            wide_ref[:, 8 * half + tile, :] = rows[:, tile * LANES:(tile + 1) * LANES]
        wide_ref[:, 8 * half + TILES, :] = jnp.zeros((OWNERS, LANES), F32)
    out_ref[0:OWNERS] = wide_ref[...].astype(BF16)
    out_ref[OWNERS:] = jnp.zeros((DEVS - OWNERS, 16, LANES), BF16)


def last_kernel(drive_ref, lrot_ref, bundle_ref, out_ref, push_ref, wide_ref):
    push = gather_push(drive_ref, lrot_ref)
    lanes = lane_ids(OWNERS)
    tiles = [
        [
            push[OWNERS * h:OWNERS * (h + 1), k * LANES:(k + 1) * LANES]
            for k in range(TILES)
        ]
        for h in range(2)
    ]
    blocks = pack_pair(tiles[0], tiles[1], lanes)
    for orbital in range(ORBS):
        push_ref[:, orbital, :] = blocks[orbital]
    square = lane_ids(HALF)
    for d in range(OWNERS):
        pair = block_diagonal(bundle_ref[d, 32:96, :].astype(F32), square).astype(BF16)
        rows = push_ref[d]
        high = rows.astype(BF16)
        low = (rows - high.astype(F32)).astype(BF16)
        push_ref[d] = TAU * (
            jnp.dot(high, pair, preferred_element_type=F32)
            + jnp.dot(low, pair, preferred_element_type=F32)
        )
    moved = [push_ref[:, orbital, :] for orbital in range(ORBS)]
    wide_ref[...] = bundle_ref[0:OWNERS, 16:32, :].astype(F32)
    for half in range(2):
        for tile in range(TILES):
            out_ref[OWNERS * half:OWNERS * (half + 1), tile * LANES:(tile + 1) * LANES] = (
                wide_ref[:, 8 * half + tile, :] + unpack_tile(moved, tile, half, lanes)
            )


def call(kernel, name, shapes, operands, in_specs, scratch=(), limit=24, micros=1.0):
    single = not isinstance(shapes, (list, tuple))
    listed = [shapes] if single else list(shapes)
    result = pl.pallas_call(
        kernel,
        out_shape=listed,
        in_specs=in_specs,
        out_specs=vmem(len(listed)),
        scratch_shapes=list(scratch),
        compiler_params=pltpu.CompilerParams(vmem_limit_bytes=limit * 1024 * 1024),
        cost_estimate=pl.CostEstimate(flops=int(micros * 1e9), bytes_accessed=0, transcendentals=0),
        name=name,
    )(*operands)
    return result[0] if single else result


def shape(dims, dtype=F32):
    return jax.ShapeDtypeStruct(dims, dtype)


def exchange(array, axis):
    flat = array.reshape(-1, LANES)
    return lax.all_to_all(flat, axis, 0, 0, tiled=True).reshape(array.shape)


def places(src_group, own_group, cap):
    source = lax.dynamic_slice_in_dim(src_group.reshape(-1), own_group * WALKERS, WALKERS)
    order = jnp.arange(WALKERS, dtype=jnp.int32)
    earlier = (source[None, :] == source[:, None]) & (order[None, :] < order[:, None])
    return source * cap + jnp.sum(earlier.astype(jnp.int32), axis=1)


def body(phi_in, trial, lrot, fields, src_group, src_slot, cap=CAP):
    groups = lax.axis_size("walk")
    own_group = lax.axis_index("walk")
    place = places(src_group, own_group, cap)
    rows = call(
        migrate_pack, "migrate_pack", shape((groups * cap, 8, LANES)),
        (own_group.reshape(1), src_group.reshape(1, -1), src_slot.reshape(1, -1), phi_in),
        smem() + vmem(3),
    )
    rows = exchange(rows, "walk")
    owned = call(
        owner_pack, "owner_pack", shape((DEVS, 24, LANES)), (place, rows, trial),
        smem() + vmem(2), [pltpu.VMEM((ORBS, LANES), F32)],
    )
    owned = exchange(owned, "chol")
    wide = pltpu.VMEM((DEVS, 16, LANES), F32)
    few = pltpu.VMEM((OWNERS, 16, LANES), F32)
    theta, phi, corr, trial_all = call(
        owner_first, "owner_first",
        [
            shape((DEVS, 16, LANES), BF16), shape((DEVS * ORBS, LANES)),
            shape((HALF, LANES)), shape((DEVS * ORBS // 2, LANES)),
        ],
        (owned,), vmem(), [wide], micros=6.0,
    )
    theta = exchange(theta, "chol")

    def forces(theta, step):
        force = call(
            force_kernel, "force", shape((DEVS, OWNERS, LANES), BF16), (theta, lrot), vmem(2), [few]
        )
        force = exchange(force, "chol")
        drive, capped = call(
            lambda *refs: drive_kernel(step, *refs), "drive",
            [shape((DEVS, OWNERS, LANES), BF16), shape((WALKERS, HALF))],
            (force, fields), vmem(2), [pltpu.VMEM((WALKERS, LANES), F32)],
        )
        return exchange(drive, "chol"), capped

    drive, _ = forces(theta, 0)
    push = call(push_kernel, "push", shape((DEVS, 16, LANES), BF16), (drive, lrot), vmem(2), [few])
    push = exchange(push, "chol")
    bundle = call(
        owner_next, "owner_next", shape((DEVS, 96, LANES), BF16),
        (push, phi, corr, trial_all), vmem(4), [wide], micros=6.0,
    )
    bundle = exchange(bundle, "chol")
    drive, capped = forces(bundle, 1)
    phi_out = call(
        last_kernel, "last", shape((WALKERS, ORBS * ELECS)), (drive, lrot, bundle), vmem(3),
        [few, few],
    )
    return phi_out, capped


def solution(mesh):
    return jax.shard_map(
        body,
        mesh=mesh,
        in_specs=(
            P("walk", "chol"),
            P("chol", None),
            P("chol", None),
            P(None, "walk", "chol"),
            P(),
            P(),
        ),
        out_specs=(P("walk", "chol"), P("walk", "chol")),
        check_vma=False,
    )
```

```python
import jax
import jax.numpy as jnp
from jax import lax
from jax.experimental import pallas as pl
from jax.experimental.pallas import tpu as pltpu
from jax.sharding import PartitionSpec as P

F32 = jnp.float32
BF16 = jnp.bfloat16
LANES = 128
HALF = 64
ELECS = 56
ORBS = 16
TILES = 7
DEVS = 32
WALKERS = 48
OWNERS = 24
CAP = 6
PANEL = 8
CHOLS = 2048
TAU = 0.03
EXACT = lax.Precision.HIGHEST


def vmem(count=1):
    return [pl.BlockSpec(memory_space=pltpu.VMEM)] * count


def smem():
    return [pl.BlockSpec(memory_space=pltpu.SMEM)]


def lane_ids(rows):
    return lax.broadcasted_iota(jnp.int32, (rows, LANES), 1)


def turn(block, shift):
    shift = shift % LANES
    return pltpu.roll(block, shift, 1) if shift else block


def exact_dot(left, right, left_dim, right_dim):
    return lax.dot_general(
        left, right, (((left_dim,), (right_dim,)), ((), ())),
        precision=EXACT, preferred_element_type=F32,
    )


def take_orbital(tiles, orbital, dest, lanes):
    tile, offset = divmod(orbital * ELECS, LANES)
    shift = dest - offset
    low = turn(tiles[tile], shift)
    if offset + ELECS <= LANES:
        return low
    return jnp.where(lanes >= dest + LANES - offset, turn(tiles[tile + 1], shift), low)


def pack_pair(first, second, lanes):
    blocks = []
    for orbital in range(ORBS):
        left = take_orbital(first, orbital, 0, lanes)
        right = take_orbital(second, orbital, HALF, lanes)
        block = jnp.where(lanes < HALF, left, right)
        blocks.append(jnp.where((lanes & (HALF - 1)) < ELECS, block, 0.0))
    return blocks


def unpack_tile(blocks, tile, half, lanes):
    start = tile * LANES
    result = None
    for orbital in range(start // ELECS, (start + LANES - 1) // ELECS + 1):
        moved = turn(blocks[orbital], orbital * ELECS - start - half * HALF)
        if result is None:
            result = moved
        else:
            result = jnp.where(lanes >= orbital * ELECS - start, moved, result)
    return result


def block_diagonal(pair, lanes):
    return jnp.concatenate(
        [jnp.where(lanes < HALF, pair, 0.0), jnp.where(lanes >= HALF, pair, 0.0)], axis=0
    )


def invert_pair(gram):
    lanes = lane_ids(ELECS)
    row_ids = lax.broadcasted_iota(jnp.int32, (ELECS, LANES), 0)
    within = lanes & (HALF - 1)
    base = lanes & HALF
    for start in range(0, ELECS, PANEL):
        columns = {
            m: jnp.take_along_axis(gram, base + m, axis=1) for m in range(start, start + PANEL)
        }
        for k in range(start, start + PANEL):
            column = columns.pop(k)
            scale = 1.0 / column[k:k + 1, :]
            row = jnp.where(within[0:1] == k, 1.0, gram[k:k + 1, :]) * scale
            for m in columns:
                entry = columns[m][k:k + 1, :] * scale
                columns[m] = jnp.where(row_ids == k, entry, columns[m] - column * entry)
            gram = jnp.where(row_ids == k, row, jnp.where(within == k, 0.0, gram) - column * row)
    return gram


def correlate(trial, walkers):
    rows = DEVS * ORBS // 2
    low = exact_dot(trial, walkers[:rows], 0, 0)
    high = exact_dot(trial, walkers[rows:], 0, 0)
    return low[:HALF] + high[HALF:]


def theta_blocks(walkers, correlation):
    lanes = lane_ids(HALF)
    gram = exact_dot(correlation, correlation, 0, 0)
    packed = jnp.where(lanes[:ELECS] < HALF, gram[:ELECS], gram[HALF:HALF + ELECS])
    inverse_gram = invert_pair(packed)
    inverse_gram = jnp.concatenate([inverse_gram, jnp.zeros((HALF - ELECS, LANES), F32)], axis=0)
    inverse = exact_dot(block_diagonal(inverse_gram, lanes), block_diagonal(correlation, lanes), 1, 1)
    theta = exact_dot(walkers, inverse, 1, 0)
    return [theta[DEVS * a:DEVS * (a + 1)] for a in range(ORBS)]


def migrate_pack(
    group_ref, source_hbm, slot_hbm, phi_hbm, out_ref, source_ref, slot_ref, phi_ref, sems
):
    pairs = ((source_hbm, source_ref), (slot_hbm, slot_ref), (phi_hbm, phi_ref))
    copies = [pltpu.make_async_copy(a, b, sems.at[i]) for i, (a, b) in enumerate(pairs)]
    for copy in copies:
        copy.start()
    copies[0].wait()
    count = source_ref.shape[1]
    groups = count // WALKERS
    cap = out_ref.shape[0] // groups
    walker = lax.broadcasted_iota(jnp.int32, (8, count), 1)
    block = lax.div(walker, WALKERS)
    place = walker - block * WALKERS
    mine = jnp.broadcast_to((source_ref[...] == group_ref[0]).astype(jnp.int32), (8, count))
    order = mine
    step = 1
    while step < WALKERS:
        order = order + jnp.where(place >= step, pltpu.roll(order, step, 1), 0)
        step *= 2
    target = jnp.where(mine == 1, block * cap + order - 1, -1)[0:1]
    row_ids = lax.broadcasted_iota(jnp.int32, (groups * cap, count), 0)
    slot_ids = lax.broadcasted_iota(jnp.int32, (WALKERS, count), 0)
    taken = jnp.where(row_ids == target, 1.0, 0.0).astype(BF16)
    copies[1].wait()
    held = jnp.where(slot_ids == slot_ref[...].reshape(1, count), 1.0, 0.0).astype(BF16)
    choice = lax.dot_general(taken, held, (((1,), (1,)), ((), ())), preferred_element_type=F32)
    copies[2].wait()
    rows = exact_dot(choice, phi_ref[...], 1, 0)
    for tile in range(TILES):
        out_ref[:, tile, :] = rows[:, tile * LANES:(tile + 1) * LANES]
    out_ref[:, TILES, :] = jnp.zeros((groups * cap, LANES), F32)


def owner_pack(place_ref, rows_ref, trial_ref, out_ref, pad_ref):
    pad_ref[...] = jnp.zeros_like(pad_ref)
    pad_ref[:, :ELECS] = trial_ref[...]
    trial = pad_ref[0:8, :] + turn(pad_ref[8:16, :], HALF)
    for d in range(DEVS):
        if d < OWNERS:
            out_ref[d, 0:8, :] = rows_ref[place_ref[d]]
            out_ref[d, 8:16, :] = rows_ref[place_ref[d + OWNERS]]
        else:
            out_ref[d, 0:16, :] = jnp.zeros((16, LANES), F32)
        out_ref[d, 16:24, :] = trial


def store_walkers(blocks, wide_ref, out_ref):
    lanes = lane_ids(DEVS)
    for half in range(2):
        for tile in range(TILES):
            wide_ref[:, 8 * half + tile, :] = unpack_tile(blocks, tile, half, lanes)
        wide_ref[:, 8 * half + TILES, :] = jnp.zeros((DEVS, LANES), F32)
    out_ref[:, 0:16, :] = wide_ref[...].astype(BF16)


def owner_first(in_ref, theta_ref, phi_ref, corr_ref, trial_ref, wide_ref):
    lanes = lane_ids(DEVS)
    tiles = [[in_ref[:, 8 * h + k, :] for k in range(TILES)] for h in range(2)]
    walkers = jnp.concatenate(pack_pair(tiles[0], tiles[1], lanes), axis=0)
    trial = jnp.concatenate([in_ref[:, 16 + k, :] for k in range(8)], axis=0)
    correlation = correlate(trial, walkers)
    phi_ref[...] = walkers
    corr_ref[...] = correlation
    trial_ref[...] = trial
    store_walkers(theta_blocks(walkers, correlation), wide_ref, theta_ref)


def owner_next(push_ref, phi_ref, corr_ref, trial_ref, out_ref, next_phi_ref, next_corr_ref, wide_ref):
    lanes = lane_ids(DEVS)
    wide_ref[...] = push_ref[...].astype(F32)
    tiles = [[wide_ref[:, 8 * h + k, :] for k in range(TILES)] for h in range(2)]
    push = jnp.concatenate(pack_pair(tiles[0], tiles[1], lanes), axis=0)
    old = block_diagonal(corr_ref[...], lane_ids(HALF))
    walkers = phi_ref[...] + TAU * exact_dot(push, old, 1, 0)
    correlation = correlate(trial_ref[...], walkers)
    next_phi_ref[...] = walkers
    next_corr_ref[...] = correlation
    store_walkers(theta_blocks(walkers, correlation), wide_ref, out_ref)
    sent = correlation[0:32].astype(BF16)
    for d in range(DEVS):
        out_ref[d, 16:48, :] = sent


def phi_pack(phi_ref, out_ref, wide_ref):
    blocks = [phi_ref[DEVS * a:DEVS * (a + 1), :] for a in range(ORBS)]
    store_walkers(blocks, wide_ref, out_ref)


def force_kernel(theta_ref, lrot_ref, *refs):
    *rest_ref, out_ref, wide_ref = refs
    rest = [ref[32:ELECS, :] for ref in rest_ref]
    wide_ref[...] = theta_ref[0:OWNERS, 0:16, :].astype(F32)
    theta = jnp.concatenate(
        [
            jnp.concatenate([wide_ref[:, 8 * h + k, :] for k in range(TILES)], axis=1)
            for h in range(2)
        ],
        axis=0,
    ).astype(BF16)
    force = jnp.dot(theta, lrot_ref[...], preferred_element_type=F32)
    lanes = lane_ids(OWNERS)
    for pair in range(DEVS // 2):
        block = force[:, pair * LANES:(pair + 1) * LANES]
        top, low = block[:OWNERS], block[OWNERS:]
        even = jnp.where(lanes < HALF, top, turn(low, HALF))
        odd = jnp.where(lanes < HALF, turn(top, HALF), low)
        out_ref[2 * pair] = jnp.concatenate([even] + rest, axis=0).astype(BF16)
        out_ref[2 * pair + 1] = jnp.concatenate([odd] + rest, axis=0).astype(BF16)


def drive_kernel(step, force_ref, fields_ref, *refs):
    *rest_ref, out_ref, capped_ref, pad_ref = refs
    total = force_ref[0].astype(F32)
    for c in range(1, DEVS):
        total = total + force_ref[c].astype(F32)
    capped = jnp.clip(20.0 * total[0:OWNERS], -1.0, 1.0)
    pad_ref[...] = jnp.zeros_like(pad_ref)
    pad_ref[:, 0:HALF] = fields_ref[step]
    lanes = lane_ids(OWNERS)
    fields = jnp.where(lanes < HALF, pad_ref[0:OWNERS, :], turn(pad_ref[OWNERS:, :], HALF))
    drive = fields - capped
    for d in range(DEVS):
        rest = [ref[d].astype(F32) for ref in rest_ref]
        out_ref[d] = jnp.concatenate([drive] + rest, axis=0).astype(BF16)
    capped_ref[0:OWNERS, :] = capped[:, 0:HALF]
    capped_ref[OWNERS:, :] = turn(capped, HALF)[:, 0:HALF]


def gather_push(drive_ref, lrot_ref):
    lanes = lane_ids(OWNERS)
    tops, lows = [], []
    for pair in range(DEVS // 2):
        left = drive_ref[2 * pair].astype(F32)[0:OWNERS]
        right = drive_ref[2 * pair + 1].astype(F32)[0:OWNERS]
        tops.append(jnp.where(lanes < HALF, left, turn(right, HALF)))
        lows.append(jnp.where(lanes < HALF, turn(left, HALF), right))
    drive = jnp.concatenate(
        [jnp.concatenate(tops, axis=1), jnp.concatenate(lows, axis=1)], axis=0
    ).astype(BF16)
    return lax.dot_general(
        drive, lrot_ref[...], (((1,), (1,)), ((), ())), preferred_element_type=F32
    )


def push_kernel(drive_ref, lrot_ref, out_ref, wide_ref):
    push = gather_push(drive_ref, lrot_ref)
    for half in range(2):
        rows = push[OWNERS * half:OWNERS * (half + 1)]
        for tile in range(TILES):
            wide_ref[:, 8 * half + tile, :] = rows[:, tile * LANES:(tile + 1) * LANES]
        wide_ref[:, 8 * half + TILES, :] = jnp.zeros((OWNERS, LANES), F32)
    out_ref[0:OWNERS] = wide_ref[...].astype(BF16)
    out_ref[OWNERS:] = jnp.zeros((DEVS - OWNERS, 16, LANES), BF16)


def last_kernel(drive_ref, lrot_ref, theta_ref, force_ref, out_ref, push_ref, wide_ref):
    push = gather_push(drive_ref, lrot_ref)
    lanes = lane_ids(OWNERS)
    tiles = [
        [
            push[OWNERS * h:OWNERS * (h + 1), k * LANES:(k + 1) * LANES]
            for k in range(TILES)
        ]
        for h in range(2)
    ]
    blocks = pack_pair(tiles[0], tiles[1], lanes)
    for orbital in range(ORBS):
        push_ref[:, orbital, :] = blocks[orbital]
    square = lane_ids(HALF)
    for d in range(OWNERS):
        pair = jnp.concatenate(
            [
                theta_ref[d, 16:48, :].astype(F32),
                force_ref[d].astype(F32)[OWNERS:],
                jnp.zeros((HALF - ELECS, LANES), F32),
            ],
            axis=0,
        )
        pair = block_diagonal(pair, square).astype(BF16)
        push_ref[d] = TAU * jnp.dot(push_ref[d].astype(BF16), pair, preferred_element_type=F32)
    moved = [push_ref[:, orbital, :] for orbital in range(ORBS)]
    for d in range(OWNERS):
        wide_ref[d] = drive_ref[d].astype(F32)[OWNERS:]
    for half in range(2):
        for tile in range(TILES):
            out_ref[OWNERS * half:OWNERS * (half + 1), tile * LANES:(tile + 1) * LANES] = (
                wide_ref[:, 8 * half + tile, :] + unpack_tile(moved, tile, half, lanes)
            )


def call(kernel, name, shapes, operands, in_specs, scratch=(), limit=24, micros=1.0):
    single = not isinstance(shapes, (list, tuple))
    listed = [shapes] if single else list(shapes)
    result = pl.pallas_call(
        kernel,
        out_shape=listed,
        in_specs=in_specs,
        out_specs=vmem(len(listed)),
        scratch_shapes=list(scratch),
        compiler_params=pltpu.CompilerParams(vmem_limit_bytes=limit * 1024 * 1024),
        cost_estimate=pl.CostEstimate(flops=int(micros * 1e9), bytes_accessed=0, transcendentals=0),
        name=name,
    )(*operands)
    return result[0] if single else result


def shape(dims, dtype=F32):
    return jax.ShapeDtypeStruct(dims, dtype)


def exchange(array, axis):
    flat = array.reshape(-1, LANES)
    return lax.all_to_all(flat, axis, 0, 0, tiled=True).reshape(array.shape)


def places(src_group, own_group, cap):
    source = lax.dynamic_slice_in_dim(src_group.reshape(-1), own_group * WALKERS, WALKERS)
    order = jnp.arange(WALKERS, dtype=jnp.int32)
    earlier = (source[None, :] == source[:, None]) & (order[None, :] < order[:, None])
    return source * cap + jnp.sum(earlier.astype(jnp.int32), axis=1)


def body(phi_in, trial, lrot, fields, src_group, src_slot, cap=CAP):
    groups = lax.axis_size("walk")
    own_group = lax.axis_index("walk")
    place = places(src_group, own_group, cap)
    rows = call(
        migrate_pack, "migrate_pack", shape((groups * cap, 8, LANES)),
        (own_group.reshape(1), src_group.reshape(1, -1), src_slot, phi_in),
        smem() + [pl.BlockSpec(memory_space=pltpu.HBM)] * 3,
        [
            pltpu.VMEM((1, groups * WALKERS), jnp.int32), pltpu.VMEM((groups * WALKERS,), jnp.int32),
            pltpu.VMEM((WALKERS, ORBS * ELECS), F32), pltpu.SemaphoreType.DMA((3,)),
        ],
        limit=60,
    )
    rows = exchange(rows, "walk")
    owned = call(
        owner_pack, "owner_pack", shape((DEVS, 24, LANES)), (place, rows, trial),
        smem() + vmem(2), [pltpu.VMEM((ORBS, LANES), F32)],
    )
    owned = exchange(owned, "chol")
    wide = pltpu.VMEM((DEVS, 16, LANES), F32)
    few = pltpu.VMEM((OWNERS, 16, LANES), F32)
    theta, phi, corr, trial_all = call(
        owner_first, "owner_first",
        [
            shape((DEVS, 16, LANES), BF16), shape((DEVS * ORBS, LANES)),
            shape((HALF, LANES)), shape((DEVS * ORBS // 2, LANES)),
        ],
        (owned,), vmem(), [wide], micros=6.0,
    )
    theta = exchange(theta, "chol")

    def forces(theta, step, corr=(), phi=()):
        force = call(
            force_kernel, "force", shape((DEVS, OWNERS + 24 * len(corr), LANES), BF16),
            (theta, lrot, *corr), vmem(2 + len(corr)), [few],
        )
        force = exchange(force, "chol")
        drive, capped = call(
            lambda *refs: drive_kernel(step, *refs), "drive",
            [shape((DEVS, OWNERS + 16 * len(phi), LANES), BF16), shape((WALKERS, HALF))],
            (force, fields, *phi), vmem(2 + len(phi)), [pltpu.VMEM((WALKERS, LANES), F32)],
        )
        return force, exchange(drive, "chol"), capped

    _, drive, _ = forces(theta, 0)
    push = call(push_kernel, "push", shape((DEVS, 16, LANES), BF16), (drive, lrot), vmem(2), [few])
    push = exchange(push, "chol")
    theta, phi, corr = call(
        owner_next, "owner_next",
        [shape((DEVS, 48, LANES), BF16), shape((DEVS * ORBS, LANES)), shape((HALF, LANES))],
        (push, phi, corr, trial_all), vmem(4), [wide], micros=6.0,
    )
    theta = exchange(theta, "chol")
    phi = call(phi_pack, "phi_pack", shape((DEVS, 16, LANES), BF16), (phi,), vmem(), [wide])
    force, drive, capped = forces(theta, 1, (corr,), (phi,))
    phi_out = call(
        last_kernel, "last", shape((WALKERS, ORBS * ELECS)), (drive, lrot, theta, force), vmem(4),
        [few, few],
    )
    return phi_out, capped


def solution(mesh):
    return jax.shard_map(
        body,
        mesh=mesh,
        in_specs=(
            P("walk", "chol"),
            P("chol", None),
            P("chol", None),
            P(None, "walk", "chol"),
            P(),
            P(),
        ),
        out_specs=(P("walk", "chol"), P("walk", "chol")),
        check_vma=False,
    )
```

```python
import jax
import jax.numpy as jnp
from jax import lax
from jax.experimental import pallas as pl
from jax.experimental.pallas import tpu as pltpu
from jax.sharding import PartitionSpec as P

F32 = jnp.float32
BF16 = jnp.bfloat16
LANES = 128
HALF = 64
ELECS = 56
ORBS = 16
TILES = 7
DEVS = 32
WALKERS = 48
OWNERS = 24
CAP = 6
PANEL = 8
CHOLS = 2048
TAU = 0.03
EXACT = lax.Precision.HIGHEST


def vmem(count=1):
    return [pl.BlockSpec(memory_space=pltpu.VMEM)] * count


def smem():
    return [pl.BlockSpec(memory_space=pltpu.SMEM)]


def lane_ids(rows):
    return lax.broadcasted_iota(jnp.int32, (rows, LANES), 1)


def turn(block, shift):
    shift = shift % LANES
    return pltpu.roll(block, shift, 1) if shift else block


def exact_dot(left, right, left_dim, right_dim):
    return lax.dot_general(
        left, right, (((left_dim,), (right_dim,)), ((), ())),
        precision=EXACT, preferred_element_type=F32,
    )


def parts(value):
    high = value.astype(BF16)
    return high, (value - high.astype(F32)).astype(BF16)


def near_dot(left, right):
    left_high, left_low = parts(left)
    right_high, right_low = parts(right)
    return jnp.dot(
        jnp.concatenate([left_high, left_high, left_low], axis=1),
        jnp.concatenate([right_high, right_low, right_high], axis=0),
        preferred_element_type=F32,
    )


def take_orbital(tiles, orbital, dest, lanes):
    tile, offset = divmod(orbital * ELECS, LANES)
    shift = dest - offset
    low = turn(tiles[tile], shift)
    if offset + ELECS <= LANES:
        return low
    return jnp.where(lanes >= dest + LANES - offset, turn(tiles[tile + 1], shift), low)


def pack_pair(first, second, lanes):
    blocks = []
    for orbital in range(ORBS):
        left = take_orbital(first, orbital, 0, lanes)
        right = take_orbital(second, orbital, HALF, lanes)
        block = jnp.where(lanes < HALF, left, right)
        blocks.append(jnp.where((lanes & (HALF - 1)) < ELECS, block, 0.0))
    return blocks


def unpack_tile(blocks, tile, half, lanes):
    start = tile * LANES
    result = None
    for orbital in range(start // ELECS, (start + LANES - 1) // ELECS + 1):
        moved = turn(blocks[orbital], orbital * ELECS - start - half * HALF)
        if result is None:
            result = moved
        else:
            result = jnp.where(lanes >= orbital * ELECS - start, moved, result)
    return result


def block_diagonal(pair, lanes):
    return jnp.concatenate(
        [jnp.where(lanes < HALF, pair, 0.0), jnp.where(lanes >= HALF, pair, 0.0)], axis=0
    )


def invert_pair(gram):
    lanes = lane_ids(ELECS)
    row_ids = lax.broadcasted_iota(jnp.int32, (ELECS, LANES), 0)
    within = lanes & (HALF - 1)
    base = lanes & HALF
    for start in range(0, ELECS, PANEL):
        columns = {
            m: jnp.take_along_axis(gram, base + m, axis=1) for m in range(start, start + PANEL)
        }
        for k in range(start, start + PANEL):
            column = columns.pop(k)
            scale = 1.0 / column[k:k + 1, :]
            row = jnp.where(within[0:1] == k, 1.0, gram[k:k + 1, :]) * scale
            for m in columns:
                entry = columns[m][k:k + 1, :] * scale
                columns[m] = jnp.where(row_ids == k, entry, columns[m] - column * entry)
            gram = jnp.where(row_ids == k, row, jnp.where(within == k, 0.0, gram) - column * row)
    return gram


def correlate(trial, walkers):
    rows = DEVS * ORBS // 2
    both = near_dot(trial, jnp.concatenate([walkers[:rows], walkers[rows:]], axis=1))
    return both[:HALF, :LANES] + both[HALF:, LANES:]


def theta_blocks(walkers, correlation):
    lanes = lane_ids(HALF)
    gram = exact_dot(correlation, correlation, 0, 0)
    packed = jnp.where(lanes[:ELECS] < HALF, gram[:ELECS], gram[HALF:HALF + ELECS])
    inverse_gram = invert_pair(packed)
    inverse_gram = jnp.concatenate([inverse_gram, jnp.zeros((HALF - ELECS, LANES), F32)], axis=0)
    inverse = exact_dot(block_diagonal(inverse_gram, lanes), block_diagonal(correlation, lanes), 1, 1)
    theta = near_dot(walkers, inverse)
    return [theta[DEVS * a:DEVS * (a + 1)] for a in range(ORBS)]


def migrate_pack(
    group_ref, source_hbm, slot_hbm, phi_hbm, out_ref, source_ref, slot_ref, phi_ref, sems
):
    pairs = ((source_hbm, source_ref), (slot_hbm, slot_ref), (phi_hbm, phi_ref))
    copies = [pltpu.make_async_copy(a, b, sems.at[i]) for i, (a, b) in enumerate(pairs)]
    for copy in copies:
        copy.start()
    copies[0].wait()
    count = source_ref.shape[1]
    groups = count // WALKERS
    cap = out_ref.shape[0] // groups
    walker = lax.broadcasted_iota(jnp.int32, (8, count), 1)
    block = lax.div(walker, WALKERS)
    place = walker - block * WALKERS
    mine = jnp.broadcast_to((source_ref[...] == group_ref[0]).astype(jnp.int32), (8, count))
    order = mine
    step = 1
    while step < WALKERS:
        order = order + jnp.where(place >= step, pltpu.roll(order, step, 1), 0)
        step *= 2
    target = jnp.where(mine == 1, block * cap + order - 1, -1)[0:1]
    row_ids = lax.broadcasted_iota(jnp.int32, (groups * cap, count), 0)
    slot_ids = lax.broadcasted_iota(jnp.int32, (WALKERS, count), 0)
    taken = jnp.where(row_ids == target, 1.0, 0.0).astype(BF16)
    copies[1].wait()
    held = jnp.where(slot_ids == slot_ref[...].reshape(1, count), 1.0, 0.0).astype(BF16)
    choice = lax.dot_general(taken, held, (((1,), (1,)), ((), ())), preferred_element_type=F32)
    copies[2].wait()
    rows = exact_dot(choice, phi_ref[...], 1, 0)
    for tile in range(TILES):
        out_ref[:, tile, :] = rows[:, tile * LANES:(tile + 1) * LANES]
    out_ref[:, TILES, :] = jnp.zeros((groups * cap, LANES), F32)


def owner_pack(place_ref, rows_ref, trial_ref, out_ref, pad_ref):
    pad_ref[...] = jnp.zeros_like(pad_ref)
    pad_ref[:, :ELECS] = trial_ref[...]
    trial = pad_ref[0:8, :] + turn(pad_ref[8:16, :], HALF)
    for d in range(DEVS):
        if d < OWNERS:
            out_ref[d, 0:8, :] = rows_ref[place_ref[d]]
            out_ref[d, 8:16, :] = rows_ref[place_ref[d + OWNERS]]
        else:
            out_ref[d, 0:16, :] = jnp.zeros((16, LANES), F32)
        out_ref[d, 16:24, :] = trial


def store_walkers(blocks, wide_ref, out_ref):
    lanes = lane_ids(DEVS)
    for half in range(2):
        for tile in range(TILES):
            wide_ref[:, 8 * half + tile, :] = unpack_tile(blocks, tile, half, lanes)
        wide_ref[:, 8 * half + TILES, :] = jnp.zeros((DEVS, LANES), F32)
    out_ref[:, 0:16, :] = wide_ref[...].astype(BF16)


def owner_first(in_ref, theta_ref, phi_ref, corr_ref, trial_ref, wide_ref):
    lanes = lane_ids(DEVS)
    tiles = [[in_ref[:, 8 * h + k, :] for k in range(TILES)] for h in range(2)]
    walkers = jnp.concatenate(pack_pair(tiles[0], tiles[1], lanes), axis=0)
    trial = jnp.concatenate([in_ref[:, 16 + k, :] for k in range(8)], axis=0).T
    correlation = correlate(trial, walkers)
    phi_ref[...] = walkers
    corr_ref[...] = correlation
    trial_ref[...] = trial
    store_walkers(theta_blocks(walkers, correlation), wide_ref, theta_ref)


def owner_next(push_ref, phi_ref, corr_ref, trial_ref, out_ref, next_phi_ref, next_corr_ref, wide_ref):
    lanes = lane_ids(DEVS)
    wide_ref[...] = push_ref[...].astype(F32)
    tiles = [[wide_ref[:, 8 * h + k, :] for k in range(TILES)] for h in range(2)]
    push = jnp.concatenate(pack_pair(tiles[0], tiles[1], lanes), axis=0)
    high, low = parts(block_diagonal(corr_ref[...], lane_ids(HALF)))
    moved = jnp.dot(
        push.astype(BF16), jnp.concatenate([high, low], axis=1), preferred_element_type=F32
    )
    walkers = phi_ref[...] + TAU * (moved[:, :LANES] + moved[:, LANES:])
    correlation = correlate(trial_ref[...], walkers)
    next_corr_ref[...] = correlation
    blocks = [walkers[DEVS * a:DEVS * (a + 1)] for a in range(ORBS)]
    store_walkers(blocks, wide_ref, next_phi_ref)
    store_walkers(theta_blocks(walkers, correlation), wide_ref, out_ref)
    sent = correlation[0:32].astype(BF16)
    for d in range(DEVS):
        out_ref[d, 16:48, :] = sent


def force_kernel(theta_ref, lrot_ref, *refs):
    *rest_ref, out_ref, wide_ref = refs
    rest = [ref[32:ELECS, :] for ref in rest_ref]
    wide_ref[...] = theta_ref[0:OWNERS, 0:16, :].astype(F32)
    theta = jnp.concatenate(
        [
            jnp.concatenate([wide_ref[:, 8 * h + k, :] for k in range(TILES)], axis=1)
            for h in range(2)
        ],
        axis=0,
    ).astype(BF16)
    force = jnp.dot(theta, lrot_ref[...], preferred_element_type=F32)
    lanes = lane_ids(OWNERS)
    for pair in range(DEVS // 2):
        block = force[:, pair * LANES:(pair + 1) * LANES]
        top, low = block[:OWNERS], block[OWNERS:]
        even = jnp.where(lanes < HALF, top, turn(low, HALF))
        odd = jnp.where(lanes < HALF, turn(top, HALF), low)
        out_ref[2 * pair] = jnp.concatenate([even] + rest, axis=0).astype(BF16)
        out_ref[2 * pair + 1] = jnp.concatenate([odd] + rest, axis=0).astype(BF16)


def drive_kernel(step, force_ref, fields_ref, *refs):
    *rest_ref, out_ref, capped_ref, pad_ref = refs
    total = force_ref[0].astype(F32)
    for c in range(1, DEVS):
        total = total + force_ref[c].astype(F32)
    capped = jnp.clip(20.0 * total[0:OWNERS], -1.0, 1.0)
    pad_ref[...] = jnp.zeros_like(pad_ref)
    pad_ref[:, 0:HALF] = fields_ref[step]
    lanes = lane_ids(OWNERS)
    fields = jnp.where(lanes < HALF, pad_ref[0:OWNERS, :], turn(pad_ref[OWNERS:, :], HALF))
    drive = fields - capped
    for d in range(DEVS):
        rest = [ref[d].astype(F32) for ref in rest_ref]
        out_ref[d] = jnp.concatenate([drive] + rest, axis=0).astype(BF16)
    capped_ref[0:OWNERS, :] = capped[:, 0:HALF]
    capped_ref[OWNERS:, :] = turn(capped, HALF)[:, 0:HALF]


def gather_push(drive_ref, lrot_ref):
    lanes = lane_ids(OWNERS)
    tops, lows = [], []
    for pair in range(DEVS // 2):
        left = drive_ref[2 * pair].astype(F32)[0:OWNERS]
        right = drive_ref[2 * pair + 1].astype(F32)[0:OWNERS]
        tops.append(jnp.where(lanes < HALF, left, turn(right, HALF)))
        lows.append(jnp.where(lanes < HALF, turn(left, HALF), right))
    drive = jnp.concatenate(
        [jnp.concatenate(tops, axis=1), jnp.concatenate(lows, axis=1)], axis=0
    ).astype(BF16)
    return lax.dot_general(
        drive, lrot_ref[...], (((1,), (1,)), ((), ())), preferred_element_type=F32
    )


def push_kernel(drive_ref, lrot_ref, out_ref, wide_ref):
    push = gather_push(drive_ref, lrot_ref)
    for half in range(2):
        rows = push[OWNERS * half:OWNERS * (half + 1)]
        for tile in range(TILES):
            wide_ref[:, 8 * half + tile, :] = rows[:, tile * LANES:(tile + 1) * LANES]
        wide_ref[:, 8 * half + TILES, :] = jnp.zeros((OWNERS, LANES), F32)
    out_ref[0:OWNERS] = wide_ref[...].astype(BF16)
    out_ref[OWNERS:] = jnp.zeros((DEVS - OWNERS, 16, LANES), BF16)


def last_kernel(drive_ref, lrot_ref, theta_ref, force_ref, out_ref, push_ref, wide_ref):
    push = gather_push(drive_ref, lrot_ref)
    lanes = lane_ids(OWNERS)
    tiles = [
        [
            push[OWNERS * h:OWNERS * (h + 1), k * LANES:(k + 1) * LANES]
            for k in range(TILES)
        ]
        for h in range(2)
    ]
    blocks = pack_pair(tiles[0], tiles[1], lanes)
    for orbital in range(ORBS):
        push_ref[:, orbital, :] = blocks[orbital]
    square = lane_ids(HALF)
    for d in range(OWNERS):
        pair = jnp.concatenate(
            [
                theta_ref[d, 16:48, :].astype(F32),
                force_ref[d].astype(F32)[OWNERS:],
                jnp.zeros((HALF - ELECS, LANES), F32),
            ],
            axis=0,
        )
        pair = block_diagonal(pair, square).astype(BF16)
        push_ref[d] = TAU * jnp.dot(push_ref[d].astype(BF16), pair, preferred_element_type=F32)
    moved = [push_ref[:, orbital, :] for orbital in range(ORBS)]
    for d in range(OWNERS):
        wide_ref[d] = drive_ref[d].astype(F32)[OWNERS:]
    for half in range(2):
        for tile in range(TILES):
            out_ref[OWNERS * half:OWNERS * (half + 1), tile * LANES:(tile + 1) * LANES] = (
                wide_ref[:, 8 * half + tile, :] + unpack_tile(moved, tile, half, lanes)
            )


def call(kernel, name, shapes, operands, in_specs, scratch=(), limit=24, micros=1.0):
    single = not isinstance(shapes, (list, tuple))
    listed = [shapes] if single else list(shapes)
    result = pl.pallas_call(
        kernel,
        out_shape=listed,
        in_specs=in_specs,
        out_specs=vmem(len(listed)),
        scratch_shapes=list(scratch),
        compiler_params=pltpu.CompilerParams(vmem_limit_bytes=limit * 1024 * 1024),
        cost_estimate=pl.CostEstimate(flops=int(micros * 1e9), bytes_accessed=0, transcendentals=0),
        name=name,
    )(*operands)
    return result[0] if single else result


def shape(dims, dtype=F32):
    return jax.ShapeDtypeStruct(dims, dtype)


def exchange(array, axis):
    flat = array.reshape(-1, LANES)
    return lax.all_to_all(flat, axis, 0, 0, tiled=True).reshape(array.shape)


def places(src_group, own_group, cap):
    source = lax.dynamic_slice_in_dim(src_group.reshape(-1), own_group * WALKERS, WALKERS)
    order = jnp.arange(WALKERS, dtype=jnp.int32)
    earlier = (source[None, :] == source[:, None]) & (order[None, :] < order[:, None])
    return source * cap + jnp.sum(earlier.astype(jnp.int32), axis=1)


def body(phi_in, trial, lrot, fields, src_group, src_slot, cap=CAP):
    groups = lax.axis_size("walk")
    own_group = lax.axis_index("walk")
    place = places(src_group, own_group, cap)
    rows = call(
        migrate_pack, "migrate_pack", shape((groups * cap, 8, LANES)),
        (own_group.reshape(1), src_group.reshape(1, -1), src_slot, phi_in),
        smem() + [pl.BlockSpec(memory_space=pltpu.HBM)] * 3,
        [
            pltpu.VMEM((1, groups * WALKERS), jnp.int32), pltpu.VMEM((groups * WALKERS,), jnp.int32),
            pltpu.VMEM((WALKERS, ORBS * ELECS), F32), pltpu.SemaphoreType.DMA((3,)),
        ],
        limit=60,
    )
    rows = exchange(rows, "walk")
    owned = call(
        owner_pack, "owner_pack", shape((DEVS, 24, LANES)), (place, rows, trial),
        smem() + vmem(2), [pltpu.VMEM((ORBS, LANES), F32)],
    )
    owned = exchange(owned, "chol")
    wide = pltpu.VMEM((DEVS, 16, LANES), F32)
    few = pltpu.VMEM((OWNERS, 16, LANES), F32)
    theta, phi, corr, trial_all = call(
        owner_first, "owner_first",
        [
            shape((DEVS, 16, LANES), BF16), shape((DEVS * ORBS, LANES)),
            shape((HALF, LANES)), shape((LANES, DEVS * ORBS // 2)),
        ],
        (owned,), vmem(), [wide], micros=6.0,
    )
    theta = exchange(theta, "chol")

    def forces(theta, step, corr=(), phi=()):
        force = call(
            force_kernel, "force", shape((DEVS, OWNERS + 24 * len(corr), LANES), BF16),
            (theta, lrot, *corr), vmem(2 + len(corr)), [few],
        )
        force = exchange(force, "chol")
        drive, capped = call(
            lambda *refs: drive_kernel(step, *refs), "drive",
            [shape((DEVS, OWNERS + 16 * len(phi), LANES), BF16), shape((WALKERS, HALF))],
            (force, fields, *phi), vmem(2 + len(phi)), [pltpu.VMEM((WALKERS, LANES), F32)],
        )
        return force, exchange(drive, "chol"), capped

    _, drive, _ = forces(theta, 0)
    push = call(push_kernel, "push", shape((DEVS, 16, LANES), BF16), (drive, lrot), vmem(2), [few])
    push = exchange(push, "chol")
    theta, phi, corr = call(
        owner_next, "owner_next",
        [shape((DEVS, 48, LANES), BF16), shape((DEVS, 16, LANES), BF16), shape((HALF, LANES))],
        (push, phi, corr, trial_all), vmem(4), [wide], micros=6.0,
    )
    theta = exchange(theta, "chol")
    force, drive, capped = forces(theta, 1, (corr,), (phi,))
    phi_out = call(
        last_kernel, "last", shape((WALKERS, ORBS * ELECS)), (drive, lrot, theta, force), vmem(4),
        [few, few],
    )
    return phi_out, capped


def solution(mesh):
    return jax.shard_map(
        body,
        mesh=mesh,
        in_specs=(
            P("walk", "chol"),
            P("chol", None),
            P("chol", None),
            P(None, "walk", "chol"),
            P(),
            P(),
        ),
        out_specs=(P("walk", "chol"), P("walk", "chol")),
        check_vma=False,
    )
```

```python
import jax
import jax.numpy as jnp
from jax import lax
from jax.experimental import pallas as pl
from jax.experimental.pallas import tpu as pltpu
from jax.sharding import PartitionSpec as P

F32 = jnp.float32
BF16 = jnp.bfloat16
LANES = 128
HALF = 64
ELECS = 56
ORBS = 16
TILES = 7
DEVS = 32
WALKERS = 48
OWNERS = 24
CAP = 6
PANEL = 8
CHOLS = 2048
TAU = 0.03
EXACT = lax.Precision.HIGHEST


def vmem(count=1):
    return [pl.BlockSpec(memory_space=pltpu.VMEM)] * count


def smem():
    return [pl.BlockSpec(memory_space=pltpu.SMEM)]


def lane_ids(rows):
    return lax.broadcasted_iota(jnp.int32, (rows, LANES), 1)


def turn(block, shift):
    shift = shift % LANES
    return pltpu.roll(block, shift, 1) if shift else block


def exact_dot(left, right, left_dim, right_dim):
    return lax.dot_general(
        left, right, (((left_dim,), (right_dim,)), ((), ())),
        precision=EXACT, preferred_element_type=F32,
    )


def parts(value):
    high = value.astype(BF16)
    return high, (value - high.astype(F32)).astype(BF16)


def near_dot(left, right):
    left_high, left_low = parts(left)
    right_high, right_low = parts(right)
    return jnp.dot(
        jnp.concatenate([left_high, left_high, left_low], axis=1),
        jnp.concatenate([right_high, right_low, right_high], axis=0),
        preferred_element_type=F32,
    )


def take_orbital(tiles, orbital, dest, lanes):
    tile, offset = divmod(orbital * ELECS, LANES)
    shift = dest - offset
    low = turn(tiles[tile], shift)
    if offset + ELECS <= LANES:
        return low
    return jnp.where(lanes >= dest + LANES - offset, turn(tiles[tile + 1], shift), low)


def pack_pair(first, second, lanes):
    blocks = []
    for orbital in range(ORBS):
        left = take_orbital(first, orbital, 0, lanes)
        right = take_orbital(second, orbital, HALF, lanes)
        block = jnp.where(lanes < HALF, left, right)
        blocks.append(jnp.where((lanes & (HALF - 1)) < ELECS, block, 0.0))
    return blocks


def unpack_tile(blocks, tile, half, lanes):
    start = tile * LANES
    result = None
    for orbital in range(start // ELECS, (start + LANES - 1) // ELECS + 1):
        moved = turn(blocks[orbital], orbital * ELECS - start - half * HALF)
        if result is None:
            result = moved
        else:
            result = jnp.where(lanes >= orbital * ELECS - start, moved, result)
    return result


def block_diagonal(pair, lanes):
    return jnp.concatenate(
        [jnp.where(lanes < HALF, pair, 0.0), jnp.where(lanes >= HALF, pair, 0.0)], axis=0
    )


def invert_pair(gram):
    lanes = lane_ids(ELECS)
    row_ids = lax.broadcasted_iota(jnp.int32, (ELECS, LANES), 0)
    within = lanes & (HALF - 1)
    base = lanes & HALF
    for start in range(0, ELECS, PANEL):
        columns = {
            m: jnp.take_along_axis(gram, base + m, axis=1) for m in range(start, start + PANEL)
        }
        for k in range(start, start + PANEL):
            column = columns.pop(k)
            scale = 1.0 / column[k:k + 1, :]
            row = jnp.where(within[0:1] == k, 1.0, gram[k:k + 1, :]) * scale
            for m in columns:
                entry = columns[m][k:k + 1, :] * scale
                columns[m] = jnp.where(row_ids == k, entry, columns[m] - column * entry)
            gram = jnp.where(row_ids == k, row, jnp.where(within == k, 0.0, gram) - column * row)
    return gram


def correlate(trial, walkers):
    rows = DEVS * ORBS // 2
    both = near_dot(trial, jnp.concatenate([walkers[:rows], walkers[rows:]], axis=1))
    return both[:HALF, :LANES] + both[HALF:, LANES:]


def theta_blocks(walkers, correlation):
    lanes = lane_ids(HALF)
    gram = exact_dot(correlation, correlation, 0, 0)
    packed = jnp.where(lanes[:ELECS] < HALF, gram[:ELECS], gram[HALF:HALF + ELECS])
    inverse_gram = invert_pair(packed)
    inverse_gram = jnp.concatenate([inverse_gram, jnp.zeros((HALF - ELECS, LANES), F32)], axis=0)
    inverse = exact_dot(block_diagonal(inverse_gram, lanes), block_diagonal(correlation, lanes), 1, 1)
    theta = near_dot(walkers, inverse)
    return [theta[DEVS * a:DEVS * (a + 1)] for a in range(ORBS)]


def migrate_pack(
    group_ref, source_hbm, slot_hbm, phi_hbm, out_ref, source_ref, slot_ref, phi_ref, sems
):
    pairs = ((source_hbm, source_ref), (slot_hbm, slot_ref), (phi_hbm, phi_ref))
    copies = [pltpu.make_async_copy(a, b, sems.at[i]) for i, (a, b) in enumerate(pairs)]
    for copy in copies:
        copy.start()
    copies[0].wait()
    count = source_ref.shape[1]
    groups = count // WALKERS
    cap = out_ref.shape[0] // groups
    walker = lax.broadcasted_iota(jnp.int32, (8, count), 1)
    block = lax.div(walker, WALKERS)
    place = walker - block * WALKERS
    mine = jnp.broadcast_to((source_ref[...] == group_ref[0]).astype(jnp.int32), (8, count))
    order = mine
    step = 1
    while step < WALKERS:
        order = order + jnp.where(place >= step, pltpu.roll(order, step, 1), 0)
        step *= 2
    target = jnp.where(mine == 1, block * cap + order - 1, -1)[0:1]
    row_ids = lax.broadcasted_iota(jnp.int32, (groups * cap, count), 0)
    slot_ids = lax.broadcasted_iota(jnp.int32, (WALKERS, count), 0)
    taken = jnp.where(row_ids == target, 1.0, 0.0).astype(BF16)
    copies[1].wait()
    held = jnp.where(slot_ids == slot_ref[...].reshape(1, count), 1.0, 0.0).astype(BF16)
    choice = lax.dot_general(taken, held, (((1,), (1,)), ((), ())), preferred_element_type=F32)
    choice = choice.astype(BF16)
    copies[2].wait()
    phi = phi_ref[...]
    high, rest = parts(phi)
    low = (phi - high.astype(F32) - rest.astype(F32)).astype(BF16)
    rows = sum(jnp.dot(choice, part, preferred_element_type=F32) for part in (high, rest, low))
    for tile in range(TILES):
        out_ref[:, tile, :] = rows[:, tile * LANES:(tile + 1) * LANES]
    out_ref[:, TILES, :] = jnp.zeros((groups * cap, LANES), F32)


def owner_pack(place_ref, rows_ref, trial_ref, out_ref, pad_ref):
    pad_ref[...] = jnp.zeros_like(pad_ref)
    pad_ref[:, :ELECS] = trial_ref[...]
    trial = pad_ref[0:8, :] + turn(pad_ref[8:16, :], HALF)
    for d in range(DEVS):
        if d < OWNERS:
            out_ref[d, 0:8, :] = rows_ref[place_ref[d]]
            out_ref[d, 8:16, :] = rows_ref[place_ref[d + OWNERS]]
        else:
            out_ref[d, 0:16, :] = jnp.zeros((16, LANES), F32)
        out_ref[d, 16:24, :] = trial


def store_walkers(blocks, wide_ref, out_ref):
    lanes = lane_ids(DEVS)
    for half in range(2):
        for tile in range(TILES):
            wide_ref[:, 8 * half + tile, :] = unpack_tile(blocks, tile, half, lanes)
        wide_ref[:, 8 * half + TILES, :] = jnp.zeros((DEVS, LANES), F32)
    out_ref[:, 0:16, :] = wide_ref[...].astype(BF16)


def owner_first(in_ref, theta_ref, phi_ref, corr_ref, trial_ref, wide_ref):
    lanes = lane_ids(DEVS)
    tiles = [[in_ref[:, 8 * h + k, :] for k in range(TILES)] for h in range(2)]
    walkers = jnp.concatenate(pack_pair(tiles[0], tiles[1], lanes), axis=0)
    trial = jnp.concatenate([in_ref[:, 16 + k, :] for k in range(8)], axis=0).T
    correlation = correlate(trial, walkers)
    phi_ref[...] = walkers
    corr_ref[...] = correlation
    trial_ref[...] = trial
    store_walkers(theta_blocks(walkers, correlation), wide_ref, theta_ref)


def owner_next(push_ref, phi_ref, corr_ref, trial_ref, out_ref, next_phi_ref, next_corr_ref, wide_ref):
    lanes = lane_ids(DEVS)
    wide_ref[...] = push_ref[...].astype(F32)
    tiles = [[wide_ref[:, 8 * h + k, :] for k in range(TILES)] for h in range(2)]
    push = jnp.concatenate(pack_pair(tiles[0], tiles[1], lanes), axis=0)
    high, low = parts(block_diagonal(corr_ref[...], lane_ids(HALF)))
    moved = jnp.dot(
        push.astype(BF16), jnp.concatenate([high, low], axis=1), preferred_element_type=F32
    )
    walkers = phi_ref[...] + TAU * (moved[:, :LANES] + moved[:, LANES:])
    correlation = correlate(trial_ref[...], walkers)
    next_corr_ref[...] = correlation
    blocks = [walkers[DEVS * a:DEVS * (a + 1)] for a in range(ORBS)]
    store_walkers(blocks, wide_ref, next_phi_ref)
    store_walkers(theta_blocks(walkers, correlation), wide_ref, out_ref)
    sent = correlation[0:32].astype(BF16)
    for d in range(DEVS):
        out_ref[d, 16:48, :] = sent


def force_kernel(theta_ref, lrot_ref, *refs):
    *rest_ref, out_ref, wide_ref = refs
    rest = [ref[32:ELECS, :] for ref in rest_ref]
    wide_ref[...] = theta_ref[0:OWNERS, 0:16, :].astype(F32)
    theta = jnp.concatenate(
        [
            jnp.concatenate([wide_ref[:, 8 * h + k, :] for k in range(TILES)], axis=1)
            for h in range(2)
        ],
        axis=0,
    ).astype(BF16)
    force = jnp.dot(theta, lrot_ref[...], preferred_element_type=F32)
    lanes = lane_ids(OWNERS)
    for pair in range(DEVS // 2):
        block = force[:, pair * LANES:(pair + 1) * LANES]
        top, low = block[:OWNERS], block[OWNERS:]
        even = jnp.where(lanes < HALF, top, turn(low, HALF))
        odd = jnp.where(lanes < HALF, turn(top, HALF), low)
        out_ref[2 * pair] = jnp.concatenate(rest + [even], axis=0).astype(BF16)
        out_ref[2 * pair + 1] = jnp.concatenate(rest + [odd], axis=0).astype(BF16)


def drive_kernel(step, force_ref, fields_ref, *refs):
    *rest_ref, out_ref, capped_ref, pad_ref = refs
    total = force_ref[0].astype(F32)
    for c in range(1, DEVS):
        total = total + force_ref[c].astype(F32)
    capped = jnp.clip(20.0 * total[-OWNERS:], -1.0, 1.0)
    pad_ref[...] = jnp.zeros_like(pad_ref)
    pad_ref[:, 0:HALF] = fields_ref[step]
    lanes = lane_ids(OWNERS)
    fields = jnp.where(lanes < HALF, pad_ref[0:OWNERS, :], turn(pad_ref[OWNERS:, :], HALF))
    drive = fields - capped
    for d in range(DEVS):
        rest = [ref[d].astype(F32) for ref in rest_ref]
        out_ref[d] = jnp.concatenate(rest + [drive], axis=0).astype(BF16)
    capped_ref[0:OWNERS, :] = capped[:, 0:HALF]
    capped_ref[OWNERS:, :] = turn(capped, HALF)[:, 0:HALF]


def gather_push(drive_ref, lrot_ref):
    lanes = lane_ids(OWNERS)
    tops, lows = [], []
    for pair in range(DEVS // 2):
        left = drive_ref[2 * pair].astype(F32)[-OWNERS:]
        right = drive_ref[2 * pair + 1].astype(F32)[-OWNERS:]
        tops.append(jnp.where(lanes < HALF, left, turn(right, HALF)))
        lows.append(jnp.where(lanes < HALF, turn(left, HALF), right))
    drive = jnp.concatenate(
        [jnp.concatenate(tops, axis=1), jnp.concatenate(lows, axis=1)], axis=0
    ).astype(BF16)
    return lax.dot_general(
        drive, lrot_ref[...], (((1,), (1,)), ((), ())), preferred_element_type=F32
    )


def push_kernel(drive_ref, lrot_ref, out_ref, wide_ref):
    push = gather_push(drive_ref, lrot_ref)
    for half in range(2):
        rows = push[OWNERS * half:OWNERS * (half + 1)]
        for tile in range(TILES):
            wide_ref[:, 8 * half + tile, :] = rows[:, tile * LANES:(tile + 1) * LANES]
        wide_ref[:, 8 * half + TILES, :] = jnp.zeros((OWNERS, LANES), F32)
    out_ref[0:OWNERS] = wide_ref[...].astype(BF16)
    out_ref[OWNERS:] = jnp.zeros((DEVS - OWNERS, 16, LANES), BF16)


def last_kernel(drive_ref, lrot_ref, theta_ref, force_ref, out_ref, push_ref, wide_ref):
    push = gather_push(drive_ref, lrot_ref)
    lanes = lane_ids(OWNERS)
    for half in range(2):
        tiles = [
            push[OWNERS * half:OWNERS * (half + 1), k * LANES:(k + 1) * LANES]
            for k in range(TILES)
        ]
        for orbital in range(ORBS):
            block = take_orbital(tiles, orbital, 0, lanes)
            push_ref[:, ORBS * half + orbital, :] = jnp.where(lanes < ELECS, block, 0.0)
    for d in range(OWNERS):
        pair = jnp.concatenate([theta_ref[d, 16:48, :], force_ref[d, 0:32, :]], axis=0)
        rows = push_ref[d][:, 0:HALF].astype(BF16)
        push_ref[d] = TAU * jnp.dot(rows, pair, preferred_element_type=F32)
    wide_ref[...] = drive_ref[0:OWNERS, 0:16, :].astype(F32)
    for half in range(2):
        moved = [push_ref[:, ORBS * half + orbital, :] for orbital in range(ORBS)]
        for tile in range(TILES):
            out_ref[OWNERS * half:OWNERS * (half + 1), tile * LANES:(tile + 1) * LANES] = (
                wide_ref[:, 8 * half + tile, :] + unpack_tile(moved, tile, half, lanes)
            )


def call(kernel, name, shapes, operands, in_specs, scratch=(), limit=24, micros=1.0):
    single = not isinstance(shapes, (list, tuple))
    listed = [shapes] if single else list(shapes)
    result = pl.pallas_call(
        kernel,
        out_shape=listed,
        in_specs=in_specs,
        out_specs=vmem(len(listed)),
        scratch_shapes=list(scratch),
        compiler_params=pltpu.CompilerParams(vmem_limit_bytes=limit * 1024 * 1024),
        cost_estimate=pl.CostEstimate(flops=int(micros * 1e9), bytes_accessed=0, transcendentals=0),
        name=name,
    )(*operands)
    return result[0] if single else result


def shape(dims, dtype=F32):
    return jax.ShapeDtypeStruct(dims, dtype)


def exchange(array, axis):
    flat = array.reshape(-1, LANES)
    return lax.all_to_all(flat, axis, 0, 0, tiled=True).reshape(array.shape)


def places(src_group, own_group, cap):
    source = lax.dynamic_slice_in_dim(src_group.reshape(-1), own_group * WALKERS, WALKERS)
    order = jnp.arange(WALKERS, dtype=jnp.int32)
    earlier = (source[None, :] == source[:, None]) & (order[None, :] < order[:, None])
    return source * cap + jnp.sum(earlier.astype(jnp.int32), axis=1)


def body(phi_in, trial, lrot, fields, src_group, src_slot, cap=CAP):
    groups = lax.axis_size("walk")
    own_group = lax.axis_index("walk")
    place = places(src_group, own_group, cap)
    rows = call(
        migrate_pack, "migrate_pack", shape((groups * cap, 8, LANES)),
        (own_group.reshape(1), src_group.reshape(1, -1), src_slot, phi_in),
        smem() + [pl.BlockSpec(memory_space=pltpu.HBM)] * 3,
        [
            pltpu.VMEM((1, groups * WALKERS), jnp.int32), pltpu.VMEM((groups * WALKERS,), jnp.int32),
            pltpu.VMEM((WALKERS, ORBS * ELECS), F32), pltpu.SemaphoreType.DMA((3,)),
        ],
        limit=60,
    )
    rows = exchange(rows, "walk")
    owned = call(
        owner_pack, "owner_pack", shape((DEVS, 24, LANES)), (place, rows, trial),
        smem() + vmem(2), [pltpu.VMEM((ORBS, LANES), F32)],
    )
    owned = exchange(owned, "chol")
    wide = pltpu.VMEM((DEVS, 16, LANES), F32)
    few = pltpu.VMEM((OWNERS, 16, LANES), F32)
    theta, phi, corr, trial_all = call(
        owner_first, "owner_first",
        [
            shape((DEVS, 16, LANES), BF16), shape((DEVS * ORBS, LANES)),
            shape((HALF, LANES)), shape((LANES, DEVS * ORBS // 2)),
        ],
        (owned,), vmem(), [wide], micros=6.0,
    )
    theta = exchange(theta, "chol")

    def forces(theta, step, corr=(), phi=()):
        force = call(
            force_kernel, "force", shape((DEVS, OWNERS + 24 * len(corr), LANES), BF16),
            (theta, lrot, *corr), vmem(2 + len(corr)), [few],
        )
        force = exchange(force, "chol")
        drive, capped = call(
            lambda *refs: drive_kernel(step, *refs), "drive",
            [shape((DEVS, OWNERS + 16 * len(phi), LANES), BF16), shape((WALKERS, HALF))],
            (force, fields, *phi), vmem(2 + len(phi)), [pltpu.VMEM((WALKERS, LANES), F32)],
        )
        return force, exchange(drive, "chol"), capped

    _, drive, _ = forces(theta, 0)
    push = call(push_kernel, "push", shape((DEVS, 16, LANES), BF16), (drive, lrot), vmem(2), [few])
    push = exchange(push, "chol")
    theta, phi, corr = call(
        owner_next, "owner_next",
        [shape((DEVS, 48, LANES), BF16), shape((DEVS, 16, LANES), BF16), shape((HALF, LANES))],
        (push, phi, corr, trial_all), vmem(4), [wide], micros=6.0,
    )
    theta = exchange(theta, "chol")
    force, drive, capped = forces(theta, 1, (corr,), (phi,))
    phi_out = call(
        last_kernel, "last", shape((WALKERS, ORBS * ELECS)), (drive, lrot, theta, force), vmem(4),
        [pltpu.VMEM((OWNERS, 2 * ORBS, LANES), F32), few],
    )
    return phi_out, capped


def solution(mesh):
    return jax.shard_map(
        body,
        mesh=mesh,
        in_specs=(
            P("walk", "chol"),
            P("chol", None),
            P("chol", None),
            P(None, "walk", "chol"),
            P(),
            P(),
        ),
        out_specs=(P("walk", "chol"), P("walk", "chol")),
        check_vma=False,
    )
```

```python
import jax
import jax.numpy as jnp
from jax import lax
from jax.experimental import pallas as pl
from jax.experimental.pallas import tpu as pltpu
from jax.sharding import PartitionSpec as P

F32 = jnp.float32
BF16 = jnp.bfloat16
LANES = 128
HALF = 64
ELECS = 56
ORBS = 16
TILES = 7
DEVS = 32
WALKERS = 48
OWNERS = 24
CAP = 6
PANEL = 8
CHOLS = 2048
TAU = 0.03
EXACT = lax.Precision.HIGHEST


def vmem(count=1):
    return [pl.BlockSpec(memory_space=pltpu.VMEM)] * count


def smem():
    return [pl.BlockSpec(memory_space=pltpu.SMEM)]


def lane_ids(rows):
    return lax.broadcasted_iota(jnp.int32, (rows, LANES), 1)


def turn(block, shift):
    shift = shift % LANES
    return pltpu.roll(block, shift, 1) if shift else block


def exact_dot(left, right, left_dim, right_dim):
    return lax.dot_general(
        left, right, (((left_dim,), (right_dim,)), ((), ())),
        precision=EXACT, preferred_element_type=F32,
    )


def parts(value):
    high = value.astype(BF16)
    return high, (value - high.astype(F32)).astype(BF16)


def near_dot(left, right):
    left_high, left_low = parts(left)
    right_high, right_low = parts(right)
    return jnp.dot(
        jnp.concatenate([left_high, left_high, left_low], axis=1),
        jnp.concatenate([right_high, right_low, right_high], axis=0),
        preferred_element_type=F32,
    )


def take_orbital(tiles, orbital, dest, lanes):
    tile, offset = divmod(orbital * ELECS, LANES)
    shift = dest - offset
    low = turn(tiles[tile], shift)
    if offset + ELECS <= LANES:
        return low
    return jnp.where(lanes >= dest + LANES - offset, turn(tiles[tile + 1], shift), low)


def pack_pair(first, second, lanes):
    blocks = []
    for orbital in range(ORBS):
        left = take_orbital(first, orbital, 0, lanes)
        right = take_orbital(second, orbital, HALF, lanes)
        block = jnp.where(lanes < HALF, left, right)
        blocks.append(jnp.where((lanes & (HALF - 1)) < ELECS, block, 0.0))
    return blocks


def unpack_tile(blocks, tile, half, lanes):
    start = tile * LANES
    result = None
    for orbital in range(start // ELECS, (start + LANES - 1) // ELECS + 1):
        moved = turn(blocks[orbital], orbital * ELECS - start - half * HALF)
        if result is None:
            result = moved
        else:
            result = jnp.where(lanes >= orbital * ELECS - start, moved, result)
    return result


def block_diagonal(pair, lanes):
    return jnp.concatenate(
        [jnp.where(lanes < HALF, pair, 0.0), jnp.where(lanes >= HALF, pair, 0.0)], axis=0
    )


def invert_pair(gram):
    lanes = lane_ids(ELECS)
    row_ids = lax.broadcasted_iota(jnp.int32, (ELECS, LANES), 0)
    within = lanes & (HALF - 1)
    base = lanes & HALF
    for start in range(0, ELECS, PANEL):
        columns = {
            m: jnp.take_along_axis(gram, base + m, axis=1) for m in range(start, start + PANEL)
        }
        for k in range(start, start + PANEL):
            column = columns.pop(k)
            scale = 1.0 / column[k:k + 1, :]
            row = jnp.where(within[0:1] == k, 1.0, gram[k:k + 1, :]) * scale
            for m in columns:
                entry = columns[m][k:k + 1, :] * scale
                columns[m] = jnp.where(row_ids == k, entry, columns[m] - column * entry)
            gram = jnp.where(row_ids == k, row, jnp.where(within == k, 0.0, gram) - column * row)
    return gram


def correlate(trial, walkers):
    rows = DEVS * ORBS // 2
    both = near_dot(trial, jnp.concatenate([walkers[:rows], walkers[rows:]], axis=1))
    return both[:HALF, :LANES] + both[HALF:, LANES:]


def theta_blocks(walkers, correlation):
    lanes = lane_ids(HALF)
    gram = exact_dot(correlation, correlation, 0, 0)
    packed = jnp.where(lanes[:ELECS] < HALF, gram[:ELECS], gram[HALF:HALF + ELECS])
    inverse_gram = invert_pair(packed)
    inverse_gram = jnp.concatenate([inverse_gram, jnp.zeros((HALF - ELECS, LANES), F32)], axis=0)
    inverse = exact_dot(block_diagonal(inverse_gram, lanes), block_diagonal(correlation, lanes), 1, 1)
    theta = near_dot(walkers, inverse)
    return [theta[DEVS * a:DEVS * (a + 1)] for a in range(ORBS)]


def migrate_pack(
    group_ref, source_hbm, slot_hbm, phi_hbm, out_ref, source_ref, slot_ref, phi_ref, sems
):
    pairs = ((source_hbm, source_ref), (slot_hbm, slot_ref), (phi_hbm, phi_ref))
    copies = [pltpu.make_async_copy(a, b, sems.at[i]) for i, (a, b) in enumerate(pairs)]
    for copy in copies:
        copy.start()
    copies[0].wait()
    count = source_ref.shape[1]
    groups = count // WALKERS
    cap = out_ref.shape[0] // groups
    walker = lax.broadcasted_iota(jnp.int32, (8, count), 1)
    block = lax.div(walker, WALKERS)
    place = walker - block * WALKERS
    mine = jnp.broadcast_to((source_ref[...] == group_ref[0]).astype(jnp.int32), (8, count))
    order = mine
    step = 1
    while step < WALKERS:
        order = order + jnp.where(place >= step, pltpu.roll(order, step, 1), 0)
        step *= 2
    target = jnp.where(mine == 1, block * cap + order - 1, -1)[0:1]
    row_ids = lax.broadcasted_iota(jnp.int32, (groups * cap, count), 0)
    slot_ids = lax.broadcasted_iota(jnp.int32, (WALKERS, count), 0)
    taken = jnp.where(row_ids == target, 1.0, 0.0).astype(BF16)
    copies[1].wait()
    held = jnp.where(slot_ids == slot_ref[...].reshape(1, count), 1.0, 0.0).astype(BF16)
    choice = lax.dot_general(taken, held, (((1,), (1,)), ((), ())), preferred_element_type=F32)
    choice = choice.astype(BF16)
    copies[2].wait()
    phi = phi_ref[...]
    high, rest = parts(phi)
    low = (phi - high.astype(F32) - rest.astype(F32)).astype(BF16)
    rows = sum(jnp.dot(choice, part, preferred_element_type=F32) for part in (high, rest, low))
    for tile in range(TILES):
        out_ref[:, tile, :] = rows[:, tile * LANES:(tile + 1) * LANES]
    out_ref[:, TILES, :] = jnp.zeros((groups * cap, LANES), F32)


def owner_pack(place_ref, rows_ref, trial_ref, out_ref, pad_ref):
    pad_ref[...] = jnp.zeros_like(pad_ref)
    pad_ref[:, :ELECS] = trial_ref[...]
    trial = pad_ref[0:8, :] + turn(pad_ref[8:16, :], HALF)
    for d in range(DEVS):
        if d < OWNERS:
            out_ref[d, 0:8, :] = rows_ref[place_ref[d]]
            out_ref[d, 8:16, :] = rows_ref[place_ref[d + OWNERS]]
        else:
            out_ref[d, 0:16, :] = jnp.zeros((16, LANES), F32)
        out_ref[d, 16:24, :] = trial


def store_walkers(blocks, wide_ref, out_ref):
    lanes = lane_ids(DEVS)
    for half in range(2):
        for tile in range(TILES):
            wide_ref[:, 8 * half + tile, :] = unpack_tile(blocks, tile, half, lanes)
        wide_ref[:, 8 * half + TILES, :] = jnp.zeros((DEVS, LANES), F32)
    out_ref[:, 0:16, :] = wide_ref[...].astype(BF16)


def owner_first(in_ref, theta_ref, phi_ref, corr_ref, trial_ref, wide_ref):
    lanes = lane_ids(DEVS)
    tiles = [[in_ref[:, 8 * h + k, :] for k in range(TILES)] for h in range(2)]
    walkers = jnp.concatenate(pack_pair(tiles[0], tiles[1], lanes), axis=0)
    trial = jnp.concatenate([in_ref[:, 16 + k, :] for k in range(8)], axis=0).T
    correlation = correlate(trial, walkers)
    phi_ref[...] = walkers
    corr_ref[...] = correlation
    trial_ref[...] = trial
    store_walkers(theta_blocks(walkers, correlation), wide_ref, theta_ref)


def owner_next(push_ref, phi_ref, corr_ref, trial_ref, out_ref, next_phi_ref, next_corr_ref, wide_ref):
    lanes = lane_ids(DEVS)
    wide_ref[...] = push_ref[...].astype(F32)
    tiles = [[wide_ref[:, 8 * h + k, :] for k in range(TILES)] for h in range(2)]
    push = jnp.concatenate(pack_pair(tiles[0], tiles[1], lanes), axis=0)
    high, low = parts(block_diagonal(corr_ref[...], lane_ids(HALF)))
    moved = jnp.dot(
        push.astype(BF16), jnp.concatenate([high, low], axis=1), preferred_element_type=F32
    )
    walkers = phi_ref[...] + TAU * (moved[:, :LANES] + moved[:, LANES:])
    correlation = correlate(trial_ref[...], walkers)
    next_corr_ref[...] = correlation
    blocks = [walkers[DEVS * a:DEVS * (a + 1)] for a in range(ORBS)]
    store_walkers(blocks, wide_ref, next_phi_ref)
    store_walkers(theta_blocks(walkers, correlation), wide_ref, out_ref)
    sent = correlation[0:32].astype(BF16)
    for d in range(DEVS):
        out_ref[d, 16:48, :] = sent


def force_kernel(theta_ref, lrot_ref, *refs):
    *rest_ref, out_ref, wide_ref = refs
    rest = [ref[32:ELECS, :] for ref in rest_ref]
    wide_ref[...] = theta_ref[0:OWNERS, 0:16, :].astype(F32)
    theta = jnp.concatenate(
        [
            jnp.concatenate([wide_ref[:, 8 * h + k, :] for k in range(TILES)], axis=1)
            for h in range(2)
        ],
        axis=0,
    ).astype(BF16)
    force = jnp.dot(theta, lrot_ref[...], preferred_element_type=F32)
    lanes = lane_ids(OWNERS)
    for pair in range(DEVS // 2):
        block = force[:, pair * LANES:(pair + 1) * LANES]
        top, low = block[:OWNERS], block[OWNERS:]
        even = jnp.where(lanes < HALF, top, turn(low, HALF))
        odd = jnp.where(lanes < HALF, turn(top, HALF), low)
        out_ref[2 * pair] = jnp.concatenate(rest + [even], axis=0).astype(BF16)
        out_ref[2 * pair + 1] = jnp.concatenate(rest + [odd], axis=0).astype(BF16)


def drive_kernel(step, force_ref, fields_ref, *refs):
    *rest_ref, out_ref, capped_ref, pad_ref = refs
    terms = [force_ref[c].astype(F32)[-OWNERS:] for c in range(DEVS)]
    while len(terms) > 1:
        terms = [terms[i] + terms[i + 1] for i in range(0, len(terms), 2)]
    capped = jnp.clip(20.0 * terms[0], -1.0, 1.0)
    pad_ref[...] = jnp.zeros_like(pad_ref)
    pad_ref[:, 0:HALF] = fields_ref[step]
    lanes = lane_ids(OWNERS)
    fields = jnp.where(lanes < HALF, pad_ref[0:OWNERS, :], turn(pad_ref[OWNERS:, :], HALF))
    drive = fields - capped
    for d in range(DEVS):
        rest = [ref[d].astype(F32) for ref in rest_ref]
        out_ref[d] = jnp.concatenate(rest + [drive], axis=0).astype(BF16)
    capped_ref[0:OWNERS, :] = capped[:, 0:HALF]
    capped_ref[OWNERS:, :] = turn(capped, HALF)[:, 0:HALF]


def gather_push(drive_ref, lrot_ref):
    lanes = lane_ids(OWNERS)
    tops, lows = [], []
    for pair in range(DEVS // 2):
        left = drive_ref[2 * pair].astype(F32)[-OWNERS:]
        right = drive_ref[2 * pair + 1].astype(F32)[-OWNERS:]
        tops.append(jnp.where(lanes < HALF, left, turn(right, HALF)))
        lows.append(jnp.where(lanes < HALF, turn(left, HALF), right))
    drive = jnp.concatenate(
        [jnp.concatenate(tops, axis=1), jnp.concatenate(lows, axis=1)], axis=0
    ).astype(BF16)
    return lax.dot_general(
        drive, lrot_ref[...], (((1,), (1,)), ((), ())), preferred_element_type=F32
    )


def push_kernel(drive_ref, lrot_ref, out_ref, wide_ref):
    push = gather_push(drive_ref, lrot_ref)
    for half in range(2):
        rows = push[OWNERS * half:OWNERS * (half + 1)]
        for tile in range(TILES):
            wide_ref[:, 8 * half + tile, :] = rows[:, tile * LANES:(tile + 1) * LANES]
        wide_ref[:, 8 * half + TILES, :] = jnp.zeros((OWNERS, LANES), F32)
    out_ref[0:OWNERS] = wide_ref[...].astype(BF16)
    out_ref[OWNERS:] = jnp.zeros((DEVS - OWNERS, 16, LANES), BF16)


def last_kernel(drive_ref, lrot_ref, theta_ref, force_ref, out_ref, push_ref, wide_ref):
    push = gather_push(drive_ref, lrot_ref)
    lanes = lane_ids(OWNERS)
    for half in range(2):
        tiles = [
            push[OWNERS * half:OWNERS * (half + 1), k * LANES:(k + 1) * LANES]
            for k in range(TILES)
        ]
        for orbital in range(ORBS):
            block = take_orbital(tiles, orbital, 0, lanes)
            push_ref[:, ORBS * half + orbital, :] = jnp.where(lanes < ELECS, block, 0.0)
    for d in range(OWNERS):
        pair = jnp.concatenate([theta_ref[d, 16:48, :], force_ref[d, 0:32, :]], axis=0)
        rows = push_ref[d][:, 0:HALF].astype(BF16)
        push_ref[d] = TAU * jnp.dot(rows, pair, preferred_element_type=F32)
    wide_ref[...] = drive_ref[0:OWNERS, 0:16, :].astype(F32)
    for half in range(2):
        moved = [push_ref[:, ORBS * half + orbital, :] for orbital in range(ORBS)]
        for tile in range(TILES):
            out_ref[OWNERS * half:OWNERS * (half + 1), tile * LANES:(tile + 1) * LANES] = (
                wide_ref[:, 8 * half + tile, :] + unpack_tile(moved, tile, half, lanes)
            )


def call(kernel, name, shapes, operands, in_specs, scratch=(), limit=24, micros=1.0):
    single = not isinstance(shapes, (list, tuple))
    listed = [shapes] if single else list(shapes)
    result = pl.pallas_call(
        kernel,
        out_shape=listed,
        in_specs=in_specs,
        out_specs=vmem(len(listed)),
        scratch_shapes=list(scratch),
        compiler_params=pltpu.CompilerParams(vmem_limit_bytes=limit * 1024 * 1024),
        cost_estimate=pl.CostEstimate(flops=int(micros * 1e9), bytes_accessed=0, transcendentals=0),
        name=name,
    )(*operands)
    return result[0] if single else result


def shape(dims, dtype=F32):
    return jax.ShapeDtypeStruct(dims, dtype)


def exchange(array, axis):
    flat = array.reshape(-1, LANES)
    return lax.all_to_all(flat, axis, 0, 0, tiled=True).reshape(array.shape)


def places(src_group, own_group, cap):
    source = lax.dynamic_slice_in_dim(src_group.reshape(-1), own_group * WALKERS, WALKERS)
    order = jnp.arange(WALKERS, dtype=jnp.int32)
    earlier = (source[None, :] == source[:, None]) & (order[None, :] < order[:, None])
    return source * cap + jnp.sum(earlier.astype(jnp.int32), axis=1)


def body(phi_in, trial, lrot, fields, src_group, src_slot, cap=CAP):
    groups = lax.axis_size("walk")
    own_group = lax.axis_index("walk")
    place = places(src_group, own_group, cap)
    rows = call(
        migrate_pack, "migrate_pack", shape((groups * cap, 8, LANES)),
        (own_group.reshape(1), src_group.reshape(1, -1), src_slot, phi_in),
        smem() + [pl.BlockSpec(memory_space=pltpu.HBM)] * 3,
        [
            pltpu.VMEM((1, groups * WALKERS), jnp.int32), pltpu.VMEM((groups * WALKERS,), jnp.int32),
            pltpu.VMEM((WALKERS, ORBS * ELECS), F32), pltpu.SemaphoreType.DMA((3,)),
        ],
        limit=60,
    )
    rows = exchange(rows, "walk")
    owned = call(
        owner_pack, "owner_pack", shape((DEVS, 24, LANES)), (place, rows, trial),
        smem() + vmem(2), [pltpu.VMEM((ORBS, LANES), F32)],
    )
    owned = exchange(owned, "chol")
    wide = pltpu.VMEM((DEVS, 16, LANES), F32)
    few = pltpu.VMEM((OWNERS, 16, LANES), F32)
    theta, phi, corr, trial_all = call(
        owner_first, "owner_first",
        [
            shape((DEVS, 16, LANES), BF16), shape((DEVS * ORBS, LANES)),
            shape((HALF, LANES)), shape((LANES, DEVS * ORBS // 2)),
        ],
        (owned,), vmem(), [wide], micros=6.0,
    )
    theta = exchange(theta, "chol")

    def forces(theta, step, corr=(), phi=()):
        force = call(
            force_kernel, "force", shape((DEVS, OWNERS + 24 * len(corr), LANES), BF16),
            (theta, lrot, *corr), vmem(2 + len(corr)), [few],
        )
        force = exchange(force, "chol")
        drive, capped = call(
            lambda *refs: drive_kernel(step, *refs), "drive",
            [shape((DEVS, OWNERS + 16 * len(phi), LANES), BF16), shape((WALKERS, HALF))],
            (force, fields, *phi), vmem(2 + len(phi)), [pltpu.VMEM((WALKERS, LANES), F32)],
        )
        return force, exchange(drive, "chol"), capped

    _, drive, _ = forces(theta, 0)
    push = call(push_kernel, "push", shape((DEVS, 16, LANES), BF16), (drive, lrot), vmem(2), [few])
    push = exchange(push, "chol")
    theta, phi, corr = call(
        owner_next, "owner_next",
        [shape((DEVS, 48, LANES), BF16), shape((DEVS, 16, LANES), BF16), shape((HALF, LANES))],
        (push, phi, corr, trial_all), vmem(4), [wide], micros=6.0,
    )
    theta = exchange(theta, "chol")
    force, drive, capped = forces(theta, 1, (corr,), (phi,))
    phi_out = call(
        last_kernel, "last", shape((WALKERS, ORBS * ELECS)), (drive, lrot, theta, force), vmem(4),
        [pltpu.VMEM((OWNERS, 2 * ORBS, LANES), F32), few],
    )
    return phi_out, capped


def solution(mesh):
    return jax.shard_map(
        body,
        mesh=mesh,
        in_specs=(
            P("walk", "chol"),
            P("chol", None),
            P("chol", None),
            P(None, "walk", "chol"),
            P(),
            P(),
        ),
        out_specs=(P("walk", "chol"), P("walk", "chol")),
        check_vma=False,
    )
```

```python
import jax
import jax.numpy as jnp
from jax import lax
from jax.experimental import pallas as pl
from jax.experimental.pallas import tpu as pltpu
from jax.sharding import PartitionSpec as P

F32 = jnp.float32
BF16 = jnp.bfloat16
LANES = 128
HALF = 64
ELECS = 56
ORBS = 16
TILES = 7
DEVS = 32
WALKERS = 48
OWNERS = 24
CAP = 6
PANEL = 8
CHOLS = 2048
TAU = 0.03
EXACT = lax.Precision.HIGHEST


def vmem(count=1):
    return [pl.BlockSpec(memory_space=pltpu.VMEM)] * count


def smem():
    return [pl.BlockSpec(memory_space=pltpu.SMEM)]


def lane_ids(rows):
    return lax.broadcasted_iota(jnp.int32, (rows, LANES), 1)


def turn(block, shift):
    shift = shift % LANES
    return pltpu.roll(block, shift, 1) if shift else block


def exact_dot(left, right, left_dim, right_dim):
    return lax.dot_general(
        left, right, (((left_dim,), (right_dim,)), ((), ())),
        precision=EXACT, preferred_element_type=F32,
    )


def parts(value):
    high = value.astype(BF16)
    return high, (value - high.astype(F32)).astype(BF16)


def near_dot(left, right):
    left_high, left_low = parts(left)
    right_high, right_low = parts(right)
    return jnp.dot(
        jnp.concatenate([left_high, left_high, left_low], axis=1),
        jnp.concatenate([right_high, right_low, right_high], axis=0),
        preferred_element_type=F32,
    )


def take_orbital(tiles, orbital, dest, lanes):
    tile, offset = divmod(orbital * ELECS, LANES)
    shift = dest - offset
    low = turn(tiles[tile], shift)
    if offset + ELECS <= LANES:
        return low
    return jnp.where(lanes >= dest + LANES - offset, turn(tiles[tile + 1], shift), low)


def pack_pair(first, second, lanes):
    blocks = []
    for orbital in range(ORBS):
        left = take_orbital(first, orbital, 0, lanes)
        right = take_orbital(second, orbital, HALF, lanes)
        block = jnp.where(lanes < HALF, left, right)
        blocks.append(jnp.where((lanes & (HALF - 1)) < ELECS, block, 0.0))
    return blocks


def unpack_tile(blocks, tile, half, lanes):
    start = tile * LANES
    result = None
    for orbital in range(start // ELECS, (start + LANES - 1) // ELECS + 1):
        moved = turn(blocks[orbital], orbital * ELECS - start - half * HALF)
        if result is None:
            result = moved
        else:
            result = jnp.where(lanes >= orbital * ELECS - start, moved, result)
    return result


def block_diagonal(pair, lanes):
    return jnp.concatenate(
        [jnp.where(lanes < HALF, pair, 0.0), jnp.where(lanes >= HALF, pair, 0.0)], axis=0
    )


def invert_pair(gram):
    lanes = lane_ids(ELECS)
    row_ids = lax.broadcasted_iota(jnp.int32, (ELECS, LANES), 0)
    within = lanes & (HALF - 1)
    base = lanes & HALF
    for start in range(0, ELECS, PANEL):
        columns = {
            m: jnp.take_along_axis(gram, base + m, axis=1) for m in range(start, start + PANEL)
        }
        for k in range(start, start + PANEL):
            column = columns.pop(k)
            scale = 1.0 / column[k:k + 1, :]
            row = jnp.where(within[0:1] == k, 1.0, gram[k:k + 1, :]) * scale
            for m in columns:
                entry = columns[m][k:k + 1, :] * scale
                columns[m] = jnp.where(row_ids == k, entry, columns[m] - column * entry)
            gram = jnp.where(row_ids == k, row, jnp.where(within == k, 0.0, gram) - column * row)
    return gram


def correlate(trial, walkers):
    rows = DEVS * ORBS // 2
    both = near_dot(trial, jnp.concatenate([walkers[:rows], walkers[rows:]], axis=1))
    return both[:HALF, :LANES] + both[HALF:, LANES:]


def theta_blocks(walkers, correlation):
    lanes = lane_ids(HALF)
    gram = exact_dot(correlation, correlation, 0, 0)
    packed = jnp.where(lanes[:ELECS] < HALF, gram[:ELECS], gram[HALF:HALF + ELECS])
    inverse_gram = invert_pair(packed)
    inverse_gram = jnp.concatenate([inverse_gram, jnp.zeros((HALF - ELECS, LANES), F32)], axis=0)
    inverse = exact_dot(block_diagonal(inverse_gram, lanes), block_diagonal(correlation, lanes), 1, 1)
    theta = near_dot(walkers, inverse)
    return [theta[DEVS * a:DEVS * (a + 1)] for a in range(ORBS)]


def migrate_pack(
    group_ref, source_hbm, slot_hbm, phi_hbm, out_hbm, source_ref, slot_ref, phi_ref, out_ref,
    sems, out_sems,
):
    pairs = ((source_hbm, source_ref), (slot_hbm, slot_ref), (phi_hbm, phi_ref))
    copies = [pltpu.make_async_copy(a, b, sems.at[i]) for i, (a, b) in enumerate(pairs)]
    for copy in copies:
        copy.start()
    copies[0].wait()
    count = source_ref.shape[1]
    groups = count // WALKERS
    cap = out_ref.shape[0] // groups
    walker = lax.broadcasted_iota(jnp.int32, (8, count), 1)
    block = lax.div(walker, WALKERS)
    place = walker - block * WALKERS
    mine = jnp.broadcast_to((source_ref[...] == group_ref[0]).astype(jnp.int32), (8, count))
    order = mine
    step = 1
    while step < WALKERS:
        order = order + jnp.where(place >= step, pltpu.roll(order, step, 1), 0)
        step *= 2
    target = jnp.where(mine == 1, block * cap + order - 1, -1)[0:1]
    row_ids = lax.broadcasted_iota(jnp.int32, (groups * cap, count), 0)
    slot_ids = lax.broadcasted_iota(jnp.int32, (WALKERS, count), 0)
    taken = jnp.where(row_ids == target, 1.0, 0.0).astype(BF16)
    copies[1].wait()
    held = jnp.where(slot_ids == slot_ref[...].reshape(1, count), 1.0, 0.0).astype(BF16)
    choice = lax.dot_general(taken, held, (((1,), (1,)), ((), ())), preferred_element_type=F32)
    copies[2].wait()
    phi = phi_ref[...]
    high, rest = parts(phi)
    low = (phi - high.astype(F32) - rest.astype(F32)).astype(BF16)
    size = out_ref.shape[0] // 2
    sends = []
    for turn_id in range(2):
        span = slice(size * turn_id, size * (turn_id + 1))
        chosen = choice[span].astype(BF16)
        rows = sum(jnp.dot(chosen, part, preferred_element_type=F32) for part in (high, rest, low))
        for tile in range(TILES):
            out_ref[span, tile, :] = rows[:, tile * LANES:(tile + 1) * LANES]
        out_ref[span, TILES, :] = jnp.zeros((size, LANES), F32)
        send = pltpu.make_async_copy(out_ref.at[span], out_hbm.at[span], out_sems.at[turn_id])
        send.start()
        sends.append(send)
    for send in sends:
        send.wait()


def owner_pack(place_ref, rows_ref, trial_ref, out_ref, pad_ref):
    pad_ref[...] = jnp.zeros_like(pad_ref)
    pad_ref[:, :ELECS] = trial_ref[...]
    trial = pad_ref[0:8, :] + turn(pad_ref[8:16, :], HALF)
    for d in range(DEVS):
        if d < OWNERS:
            out_ref[d, 0:8, :] = rows_ref[place_ref[d]]
            out_ref[d, 8:16, :] = rows_ref[place_ref[d + OWNERS]]
        else:
            out_ref[d, 0:16, :] = jnp.zeros((16, LANES), F32)
        out_ref[d, 16:24, :] = trial


def store_walkers(blocks, wide_ref, out_ref):
    lanes = lane_ids(DEVS)
    for half in range(2):
        for tile in range(TILES):
            wide_ref[:, 8 * half + tile, :] = unpack_tile(blocks, tile, half, lanes)
        wide_ref[:, 8 * half + TILES, :] = jnp.zeros((DEVS, LANES), F32)
    out_ref[:, 0:16, :] = wide_ref[...].astype(BF16)


def owner_first(in_ref, theta_ref, phi_ref, corr_ref, trial_ref, wide_ref):
    lanes = lane_ids(DEVS)
    tiles = [[in_ref[:, 8 * h + k, :] for k in range(TILES)] for h in range(2)]
    walkers = jnp.concatenate(pack_pair(tiles[0], tiles[1], lanes), axis=0)
    trial = jnp.concatenate([in_ref[:, 16 + k, :] for k in range(8)], axis=0).T
    correlation = correlate(trial, walkers)
    phi_ref[...] = walkers
    corr_ref[...] = correlation
    trial_ref[...] = trial
    store_walkers(theta_blocks(walkers, correlation), wide_ref, theta_ref)


def owner_next(push_ref, phi_ref, corr_ref, trial_ref, out_ref, next_phi_ref, next_corr_ref, wide_ref):
    lanes = lane_ids(DEVS)
    wide_ref[...] = push_ref[...].astype(F32)
    tiles = [[wide_ref[:, 8 * h + k, :] for k in range(TILES)] for h in range(2)]
    push = jnp.concatenate(pack_pair(tiles[0], tiles[1], lanes), axis=0)
    high, low = parts(block_diagonal(corr_ref[...], lane_ids(HALF)))
    moved = jnp.dot(
        push.astype(BF16), jnp.concatenate([high, low], axis=1), preferred_element_type=F32
    )
    walkers = phi_ref[...] + TAU * (moved[:, :LANES] + moved[:, LANES:])
    correlation = correlate(trial_ref[...], walkers)
    next_corr_ref[...] = correlation
    blocks = [walkers[DEVS * a:DEVS * (a + 1)] for a in range(ORBS)]
    store_walkers(blocks, wide_ref, next_phi_ref)
    store_walkers(theta_blocks(walkers, correlation), wide_ref, out_ref)
    sent = correlation[0:32].astype(BF16)
    for d in range(DEVS):
        out_ref[d, 16:48, :] = sent


def force_kernel(theta_ref, lrot_ref, *refs):
    *rest_ref, out_ref, wide_ref = refs
    rest = [ref[32:ELECS, :] for ref in rest_ref]
    wide_ref[...] = theta_ref[0:OWNERS, 0:16, :].astype(F32)
    theta = jnp.concatenate(
        [
            jnp.concatenate([wide_ref[:, 8 * h + k, :] for k in range(TILES)], axis=1)
            for h in range(2)
        ],
        axis=0,
    ).astype(BF16)
    force = jnp.dot(theta, lrot_ref[...], preferred_element_type=F32)
    lanes = lane_ids(OWNERS)
    for pair in range(DEVS // 2):
        block = force[:, pair * LANES:(pair + 1) * LANES]
        top, low = block[:OWNERS], block[OWNERS:]
        even = jnp.where(lanes < HALF, top, turn(low, HALF))
        odd = jnp.where(lanes < HALF, turn(top, HALF), low)
        out_ref[2 * pair] = jnp.concatenate(rest + [even], axis=0).astype(BF16)
        out_ref[2 * pair + 1] = jnp.concatenate(rest + [odd], axis=0).astype(BF16)


def drive_kernel(step, force_ref, fields_ref, *refs):
    *rest_ref, out_ref, capped_ref, pad_ref = refs
    total = force_ref[0].astype(F32)
    for c in range(1, DEVS):
        total = total + force_ref[c].astype(F32)
    capped = jnp.clip(20.0 * total[-OWNERS:], -1.0, 1.0)
    pad_ref[...] = jnp.zeros_like(pad_ref)
    pad_ref[:, 0:HALF] = fields_ref[step]
    lanes = lane_ids(OWNERS)
    fields = jnp.where(lanes < HALF, pad_ref[0:OWNERS, :], turn(pad_ref[OWNERS:, :], HALF))
    drive = fields - capped
    for d in range(DEVS):
        rest = [ref[d].astype(F32) for ref in rest_ref]
        out_ref[d] = jnp.concatenate(rest + [drive], axis=0).astype(BF16)
    capped_ref[0:OWNERS, :] = capped[:, 0:HALF]
    capped_ref[OWNERS:, :] = turn(capped, HALF)[:, 0:HALF]


def gather_push(drive_ref, lrot_ref):
    lanes = lane_ids(OWNERS)
    tops, lows = [], []
    for pair in range(DEVS // 2):
        left = drive_ref[2 * pair].astype(F32)[-OWNERS:]
        right = drive_ref[2 * pair + 1].astype(F32)[-OWNERS:]
        tops.append(jnp.where(lanes < HALF, left, turn(right, HALF)))
        lows.append(jnp.where(lanes < HALF, turn(left, HALF), right))
    drive = jnp.concatenate(
        [jnp.concatenate(tops, axis=1), jnp.concatenate(lows, axis=1)], axis=0
    ).astype(BF16)
    return lax.dot_general(
        drive, lrot_ref[...], (((1,), (1,)), ((), ())), preferred_element_type=F32
    )


def push_kernel(drive_ref, lrot_ref, out_ref, wide_ref):
    push = gather_push(drive_ref, lrot_ref)
    for half in range(2):
        rows = push[OWNERS * half:OWNERS * (half + 1)]
        for tile in range(TILES):
            wide_ref[:, 8 * half + tile, :] = rows[:, tile * LANES:(tile + 1) * LANES]
        wide_ref[:, 8 * half + TILES, :] = jnp.zeros((OWNERS, LANES), F32)
    out_ref[0:OWNERS] = wide_ref[...].astype(BF16)
    out_ref[OWNERS:] = jnp.zeros((DEVS - OWNERS, 16, LANES), BF16)


def last_kernel(drive_ref, lrot_ref, theta_ref, force_ref, out_ref, push_ref, wide_ref):
    push = gather_push(drive_ref, lrot_ref)
    lanes = lane_ids(OWNERS)
    for half in range(2):
        tiles = [
            push[OWNERS * half:OWNERS * (half + 1), k * LANES:(k + 1) * LANES]
            for k in range(TILES)
        ]
        for orbital in range(ORBS):
            block = take_orbital(tiles, orbital, 0, lanes)
            push_ref[:, ORBS * half + orbital, :] = jnp.where(lanes < ELECS, block, 0.0)
    for d in range(OWNERS):
        pair = jnp.concatenate([theta_ref[d, 16:48, :], force_ref[d, 0:32, :]], axis=0)
        rows = push_ref[d][:, 0:HALF].astype(BF16)
        push_ref[d] = TAU * jnp.dot(rows, pair, preferred_element_type=F32)
    wide_ref[...] = drive_ref[0:OWNERS, 0:16, :].astype(F32)
    for half in range(2):
        moved = [push_ref[:, ORBS * half + orbital, :] for orbital in range(ORBS)]
        for tile in range(TILES):
            out_ref[OWNERS * half:OWNERS * (half + 1), tile * LANES:(tile + 1) * LANES] = (
                wide_ref[:, 8 * half + tile, :] + unpack_tile(moved, tile, half, lanes)
            )


def call(kernel, name, shapes, operands, in_specs, scratch=(), limit=24, micros=1.0, out_space=pltpu.VMEM):
    single = not isinstance(shapes, (list, tuple))
    listed = [shapes] if single else list(shapes)
    result = pl.pallas_call(
        kernel,
        out_shape=listed,
        in_specs=in_specs,
        out_specs=[pl.BlockSpec(memory_space=out_space)] * len(listed),
        scratch_shapes=list(scratch),
        compiler_params=pltpu.CompilerParams(vmem_limit_bytes=limit * 1024 * 1024),
        cost_estimate=pl.CostEstimate(flops=int(micros * 1e9), bytes_accessed=0, transcendentals=0),
        name=name,
    )(*operands)
    return result[0] if single else result


def shape(dims, dtype=F32):
    return jax.ShapeDtypeStruct(dims, dtype)


def exchange(array, axis):
    flat = array.reshape(-1, LANES)
    return lax.all_to_all(flat, axis, 0, 0, tiled=True).reshape(array.shape)


def places(src_group, own_group, cap):
    source = lax.dynamic_slice_in_dim(src_group.reshape(-1), own_group * WALKERS, WALKERS)
    order = jnp.arange(WALKERS, dtype=jnp.int32)
    earlier = (source[None, :] == source[:, None]) & (order[None, :] < order[:, None])
    return source * cap + jnp.sum(earlier.astype(jnp.int32), axis=1)


def body(phi_in, trial, lrot, fields, src_group, src_slot, cap=CAP):
    groups = lax.axis_size("walk")
    own_group = lax.axis_index("walk")
    place = places(src_group, own_group, cap)
    rows = call(
        migrate_pack, "migrate_pack", shape((groups * cap, 8, LANES)),
        (own_group.reshape(1), src_group.reshape(1, -1), src_slot, phi_in),
        smem() + [pl.BlockSpec(memory_space=pltpu.HBM)] * 3,
        [
            pltpu.VMEM((1, groups * WALKERS), jnp.int32), pltpu.VMEM((groups * WALKERS,), jnp.int32),
            pltpu.VMEM((WALKERS, ORBS * ELECS), F32), pltpu.VMEM((groups * cap, 8, LANES), F32),
            pltpu.SemaphoreType.DMA((3,)), pltpu.SemaphoreType.DMA((2,)),
        ],
        limit=60, out_space=pltpu.HBM,
    )
    rows = exchange(rows, "walk")
    owned = call(
        owner_pack, "owner_pack", shape((DEVS, 24, LANES)), (place, rows, trial),
        smem() + vmem(2), [pltpu.VMEM((ORBS, LANES), F32)],
    )
    owned = exchange(owned, "chol")
    wide = pltpu.VMEM((DEVS, 16, LANES), F32)
    few = pltpu.VMEM((OWNERS, 16, LANES), F32)
    theta, phi, corr, trial_all = call(
        owner_first, "owner_first",
        [
            shape((DEVS, 16, LANES), BF16), shape((DEVS * ORBS, LANES)),
            shape((HALF, LANES)), shape((LANES, DEVS * ORBS // 2)),
        ],
        (owned,), vmem(), [wide], micros=6.0,
    )
    theta = exchange(theta, "chol")

    def forces(theta, step, corr=(), phi=()):
        force = call(
            force_kernel, "force", shape((DEVS, OWNERS + 24 * len(corr), LANES), BF16),
            (theta, lrot, *corr), vmem(2 + len(corr)), [few],
        )
        force = exchange(force, "chol")
        drive, capped = call(
            lambda *refs: drive_kernel(step, *refs), "drive",
            [shape((DEVS, OWNERS + 16 * len(phi), LANES), BF16), shape((WALKERS, HALF))],
            (force, fields, *phi), vmem(2 + len(phi)), [pltpu.VMEM((WALKERS, LANES), F32)],
        )
        return force, exchange(drive, "chol"), capped

    _, drive, _ = forces(theta, 0)
    push = call(push_kernel, "push", shape((DEVS, 16, LANES), BF16), (drive, lrot), vmem(2), [few])
    push = exchange(push, "chol")
    theta, phi, corr = call(
        owner_next, "owner_next",
        [shape((DEVS, 48, LANES), BF16), shape((DEVS, 16, LANES), BF16), shape((HALF, LANES))],
        (push, phi, corr, trial_all), vmem(4), [wide], micros=6.0,
    )
    theta = exchange(theta, "chol")
    force, drive, capped = forces(theta, 1, (corr,), (phi,))
    phi_out = call(
        last_kernel, "last", shape((WALKERS, ORBS * ELECS)), (drive, lrot, theta, force), vmem(4),
        [pltpu.VMEM((OWNERS, 2 * ORBS, LANES), F32), few],
    )
    return phi_out, capped


def solution(mesh):
    return jax.shard_map(
        body,
        mesh=mesh,
        in_specs=(
            P("walk", "chol"),
            P("chol", None),
            P("chol", None),
            P(None, "walk", "chol"),
            P(),
            P(),
        ),
        out_specs=(P("walk", "chol"), P("walk", "chol")),
        check_vma=False,
    )
```
